768 devices in a mesh: dp: 12 (over z), fsdp: 64 (over x, y, core).
Axes of the slice: x: 4, y: 8, z: 12, core: 2. Of those that a mesh axis runs over, the one named last changes fastest.
Arguments:
- item_hidden: bfloat16 [49152, 2048], P(('dp', 'fsdp')), may hold values from -400 to 400
- item_gain: float32 [2048], replicated, may hold values from 0.25 to 1.75
- history: int32 [98304], P(('dp', 'fsdp')), may hold values from 0 to 767, as said below
- owner_map: int32 [64, 768], P('fsdp'), may hold values from 0 to 767, as said below
- user_gain: float32 [2048], replicated, may hold values from 0.25 to 1.75
- value_weight: bfloat16 [2048, 2048], P('fsdp'), may hold values from -0.125 to 0.125
- value_grad: bfloat16 [98304, 2048], P(('dp', 'fsdp')), may hold values from -6 to 6
Outputs:
- values: bfloat16 [98304, 2048], P(('dp', 'fsdp'))
- item_grad: float32 [49152, 2048], P(('dp', 'fsdp'))
The draws below stay inside these ranges and needn't reach their ends.
Inputs may be any that keep to these rules, and one draw needn't show every extreme that they name: `history`: storage row s of catalog c is row s % 64 of the items on dp index s // 64 and fsdp index c. In each aligned block of 128 positions, the positions name at most 8 distinct items stored on any one dp index, and exactly 8 for some dp index. `owner_map`: each row is a permutation.
All inputs are finite; a program needn't handle non-finite values.
Results may differ from the reference program's by a relative error of at most 0.0057.
Values may be sent and summed in bfloat16 or wider, within the bound.
No kernel may reach another device: no remote copies, remote signals or barrier semaphores. Data moves between devices by JAX's collectives and lax.ppermute only.
A program may use at most 32 MiB of HBM per device.

```python
import math
import jax
import jax.numpy as jnp
from jax import lax

D = 2048
CAP = 8
ITEM_DEV = 64
HIST_DEV = 128
KVW = 2048
ITEMS = 49152
POSITIONS = 98304
N_DP = 12
N_FSDP = 64


def owner_table(key):
    keys = jax.random.split(jax.random.fold_in(key, 11), N_FSDP)
    return jax.vmap(lambda single: jax.random.permutation(single, ITEM_DEV * N_DP))(keys).astype(jnp.int32)


def draw_owner_map(key, part):
    table = owner_table(key)
    return table


def draw_history(key, part):
    table = owner_table(key)
    key = jax.random.fold_in(key, 5)
    blocks = N_DP * N_FSDP
    first_key, second_key, third_key, fourth_key, fifth_key = jax.random.split(key, 5)
    counts = jax.random.randint(first_key, (blocks, N_DP), max(CAP // 2, 1), CAP + 1)
    fullest = jax.random.randint(second_key, (blocks,), 0, N_DP)
    counts = jnp.where(jnp.arange(N_DP)[None, :] == fullest[:, None], CAP, counts)
    perm_keys = jax.random.split(third_key, blocks * N_DP)
    ranks = jax.vmap(lambda single: jax.random.permutation(single, ITEM_DEV))(perm_keys).reshape(blocks, N_DP, ITEM_DEV)
    chosen = (ranks < counts[:, :, None]).reshape(blocks, N_DP * ITEM_DEV)
    order = jnp.argsort(jnp.where(chosen, 0, 1), axis=1, stable=True).astype(jnp.int32)
    total = jnp.sum(counts, axis=1)
    place = jnp.arange(HIST_DEV)[None, :]
    one_pick = jax.random.randint(fourth_key, (blocks, HIST_DEV), 0, 1 << 20) % total[:, None]
    two_pick = jax.random.randint(fifth_key, (blocks, HIST_DEV), 0, 1 << 20) % total[:, None]
    pick = jnp.where(place < total[:, None], place, jnp.minimum(one_pick, two_pick))
    stored = jnp.take_along_axis(order, pick, axis=1)
    column = jnp.arange(blocks) % N_FSDP
    inverse = jnp.argsort(table, axis=1, stable=True).astype(jnp.int32)
    items = jnp.take_along_axis(inverse[column], stored, axis=1)
    return items.reshape(-1).astype(jnp.int32)


def draw_item_hidden(key, part):
    key = jax.random.fold_in(key, 7)
    row_key, col_key, base_key = jax.random.split(key, 3)
    rows = jnp.exp(jax.random.uniform(row_key, (ITEMS, 1), jnp.float32, 0.0, math.log(10.0)))
    cols = jnp.exp(jax.random.uniform(col_key, (1, D), jnp.float32, 0.0, math.log(10.0)))
    base = jnp.clip(jax.random.normal(base_key, (ITEMS, D), jnp.float32), -4.0, 4.0)
    return (base * rows * cols).astype(jnp.bfloat16)


def steps_of(stream_key, dims, pieces, smallest, largest):
    factor_of = 1.0
    for axis_at, parts in pieces:
        heights = jax.random.uniform(jax.random.fold_in(jax.random.fold_in(stream_key, 6), axis_at), (parts,), jnp.float32, smallest / len(pieces), largest / len(pieces))
        factor_of = factor_of * jnp.repeat(jnp.exp(heights), dims[axis_at] // parts).reshape((-1,) + (1,) * (len(dims) - 1 - axis_at))
    return factor_of


def scatter_about(key, dims, spread, limit, cuts=(), kind=jnp.bfloat16):
    result = spread * jax.random.normal(key, dims, jnp.float32)
    if cuts:
        result = result * steps_of(key, dims, cuts, -0.22, 0.18)
    return jnp.clip(result, -limit, limit).astype(kind)


def setup_inputs(seed: int = 0) -> dict:
    streams_of = jax.random.split(jax.random.key(seed), 8)
    return {
        "item_hidden": draw_item_hidden(jax.random.fold_in(streams_of[7], 71), 0),
        "item_gain": jnp.clip(1.0 + 0.15 * jax.random.normal(streams_of[1], (D,), jnp.float32), 0.25, 1.75),
        "history": draw_history(jax.random.fold_in(streams_of[7], 71), 0),
        "owner_map": draw_owner_map(jax.random.fold_in(streams_of[7], 71), 0),
        "user_gain": jnp.clip(1.0 + 0.15 * jax.random.normal(streams_of[4], (D,), jnp.float32), 0.25, 1.75),
        "value_weight": scatter_about(streams_of[5], (D, KVW), D ** -0.5, 0.125, ((0, 64),)),
        "value_grad": scatter_about(streams_of[6], (POSITIONS, KVW), 1.0, 6.0, ((0, 768),)),
    }


eps = 1e-06

def norm_rows(values, gain):
    scale = lax.rsqrt(lax.optimization_barrier(jnp.mean(values * values, axis=1, keepdims=True)) + eps)
    return (values * scale * gain, scale)

def norm_back(values, gain, scale, upstream):
    unit = values * scale
    scaled = upstream * gain
    return scale * (scaled - unit * lax.optimization_barrier(jnp.mean(scaled * unit, axis=1, keepdims=True)))

def reference(item_hidden, item_gain, history, owner_map, user_gain, value_weight, value_grad):
    hidden = item_hidden.astype(jnp.float32)
    item_emb, item_scale = norm_rows(hidden, item_gain)
    item_emb = item_emb.astype(jnp.bfloat16)
    blocks = N_DP * N_FSDP
    hist = history.reshape(blocks, HIST_DEV)
    grads = value_grad.reshape(blocks, HIST_DEV, KVW)
    lower = jnp.arange(HIST_DEV, dtype=jnp.int32)[:, None] > jnp.arange(HIST_DEV, dtype=jnp.int32)[None, :]

    def one_block(total, inputs):
        ids, upstream_rows, block = inputs
        column = block % N_FSDP
        stored = jnp.take(owner_map[column], ids).astype(jnp.int32)
        rows = (stored // ITEM_DEV * N_FSDP + column) * ITEM_DEV + stored % ITEM_DEV
        x = jnp.take(item_emb, rows, axis=0).astype(jnp.float32)
        normed, scale = norm_rows(x, user_gain)
        normed = normed.astype(jnp.bfloat16)
        values = jnp.dot(normed, value_weight, preferred_element_type=jnp.float32).astype(jnp.bfloat16)
        upstream = jnp.dot(upstream_rows, value_weight.T, preferred_element_type=jnp.float32)
        dx = norm_back(x, user_gain, scale, upstream)
        same = rows[:, None] == rows[None, :]
        sums = jnp.dot(same.astype(jnp.float32), dx, precision=lax.Precision.HIGHEST, preferred_element_type=jnp.float32)
        sums = lax.optimization_barrier(sums.astype(jnp.bfloat16)).astype(jnp.float32)
        first = jnp.logical_not(jnp.any(same & lower, axis=1))
        contrib = jnp.where(first[:, None], sums, 0.0)
        total = total.at[rows].add(contrib)
        return (total, values)
    total, values = lax.scan(one_block, jnp.zeros((ITEMS, D), jnp.float32), (hist, grads, jnp.arange(blocks, dtype=jnp.int32)))
    item_grad = norm_back(hidden, item_gain, item_scale, total)
    return (values.reshape(POSITIONS, KVW), item_grad)
```

```python
import jax
import jax.numpy as jnp
from jax import lax
from jax.sharding import PartitionSpec as P

CAP = 8


eps = 1e-06


def norm_rows(values, gain):
    scale = lax.rsqrt(jnp.mean(values * values, axis=1, keepdims=True) + eps)
    return (values * scale * gain, scale)


def norm_back(values, gain, scale, upstream):
    unit = values * scale
    scaled = upstream * gain
    return scale * (scaled - unit * jnp.mean(scaled * unit, axis=1, keepdims=True))


def locate(owner_row, items):
    matches = items[:, None] == lax.broadcasted_iota(
        jnp.int32, (items.shape[0], owner_row.shape[0]), 1
    )
    return jnp.sum(jnp.where(matches, owner_row[None, :], 0), axis=1)


def local(item_hidden, item_gain, history, owner_map, user_gain, value_weight, value_grad):
    groups = lax.axis_size("dp")
    here = lax.axis_index("dp")
    item_rows = item_hidden.shape[0]
    hist_rows = history.shape[0]
    width = item_hidden.shape[1]
    owner_row = owner_map[0]
    pool = owner_row.shape[0]
    whole = lax.all_gather(value_weight, "fsdp", axis=0, tiled=True)
    all_history = lax.all_gather(history, "dp", axis=0, tiled=True)
    hidden = item_hidden.astype(jnp.float32)
    item_emb, item_scale = norm_rows(hidden, item_gain)
    item_emb = item_emb.astype(jnp.bfloat16)
    stored = locate(owner_row, history)
    pick = stored[:, None] == lax.broadcasted_iota(jnp.int32, (hist_rows, pool), 1)
    own_wanted = jnp.any(pick, axis=0).reshape(groups, item_rows)
    own_slot = (jnp.cumsum(own_wanted.astype(jnp.int32), axis=1) - 1).reshape(pool)
    slot_pos = jnp.sum(jnp.where(pick, own_slot[None, :], 0), axis=1)
    buffer_row = stored // item_rows * CAP + slot_pos
    one_hot = (
        buffer_row[:, None] == lax.broadcasted_iota(jnp.int32, (hist_rows, groups * CAP), 1)
    ).astype(jnp.bfloat16)
    grad_sums = lax.dot_general(
        one_hot, value_grad, (((0,), (0,)), ((), ())), preferred_element_type=jnp.float32
    ).astype(jnp.bfloat16).reshape(groups, CAP, width)
    stored_all = locate(owner_row, all_history).reshape(groups, hist_rows)
    local_rows = lax.broadcasted_iota(jnp.int32, (groups, hist_rows, item_rows), 2)
    wanted = jnp.any(stored_all[:, :, None] == here * item_rows + local_rows, axis=1)
    slot = jnp.cumsum(wanted.astype(jnp.int32), axis=1) - 1
    slot_ids = lax.broadcasted_iota(jnp.int32, (groups, CAP, item_rows), 1)
    select = (wanted[:, None, :] & (slot[:, None, :] == slot_ids)).astype(jnp.bfloat16)
    outgoing = jnp.einsum(
        "dcr,rk->dck", select, item_emb, preferred_element_type=jnp.float32
    ).astype(jnp.bfloat16)
    arrived = lax.all_to_all(
        jnp.concatenate([outgoing, grad_sums], axis=1), "dp", split_axis=0, concat_axis=0, tiled=True
    )
    incoming = arrived[:, :CAP].reshape(groups * CAP, width)
    returned = arrived[:, CAP:]
    normed, _ = norm_rows(incoming.astype(jnp.float32), user_gain)
    normed = jnp.dot(
        one_hot, normed.astype(jnp.bfloat16), preferred_element_type=jnp.float32
    ).astype(jnp.bfloat16)
    total = jnp.einsum("dcr,dck->rk", select, returned, preferred_element_type=jnp.float32)
    high = lax.reduce_precision(total, 8, 7)
    both = jnp.concatenate([high, total - high], axis=0).astype(jnp.bfloat16)
    normed, both = lax.optimization_barrier((normed, both))
    values = jnp.dot(normed, whole, preferred_element_type=jnp.float32).astype(jnp.bfloat16)
    upstream = lax.dot_general(
        both, whole, (((1,), (1,)), ((), ())), preferred_element_type=jnp.float32
    )
    upstream = upstream[:item_rows] + upstream[item_rows:]
    x = item_emb.astype(jnp.float32)
    scale = lax.rsqrt(jnp.mean(x * x, axis=1, keepdims=True) + eps)
    emb_grad = norm_back(x, user_gain, scale, upstream)
    item_grad = norm_back(hidden, item_gain, item_scale, emb_grad)
    return (values, item_grad)


def solution(mesh):
    in_specs = (
        P(("dp", "fsdp"), None),
        P(),
        P(("dp", "fsdp")),
        P("fsdp", None),
        P(),
        P("fsdp", None),
        P(("dp", "fsdp"), None),
    )
    out_specs = (P(("dp", "fsdp"), None), P(("dp", "fsdp"), None))
    return jax.shard_map(local, mesh=mesh, in_specs=in_specs, out_specs=out_specs, check_vma=False)
```

```python
import jax
import jax.numpy as jnp
from jax import lax
from jax.sharding import Mesh, PartitionSpec as P

CAP = 8
NX, NY, NCORE = 4, 8, 2
ROW = ("x", "y", "core")


eps = 1e-06


def norm_rows(values, gain):
    scale = lax.rsqrt(jnp.mean(values * values, axis=1, keepdims=True) + eps)
    return (values * scale * gain, scale)


def norm_back(values, gain, scale, upstream):
    unit = values * scale
    scaled = upstream * gain
    return scale * (scaled - unit * jnp.mean(scaled * unit, axis=1, keepdims=True))


def locate(owner_row, items):
    matches = items[:, None] == lax.broadcasted_iota(
        jnp.int32, (items.shape[0], owner_row.shape[0]), 1
    )
    return jnp.sum(jnp.where(matches, owner_row[None, :], 0), axis=1)


def dot(a, b, da=1, db=0):
    return lax.dot_general(a, b, (((da,), (db,)), ((), ())), preferred_element_type=jnp.float32)


def shift(a, axis, step):
    n = lax.axis_size(axis)
    return lax.ppermute(a, axis, [((i + step) % n, i) for i in range(n)])


def turned(a, start):
    twice = jnp.concatenate([a, a], axis=1)
    return lax.dynamic_slice_in_dim(twice, start, a.shape[1], axis=1)


def local(item_hidden, item_gain, history, owner_map, user_gain, value_weight, value_grad):
    groups = lax.axis_size("dp")
    item_rows, width = item_hidden.shape
    hist_rows = history.shape[0]
    half = width // 2
    block = width // NX
    core = lax.axis_index("core")
    color = (lax.axis_index("x") + 2 * (lax.axis_index("dp") % 2)) % NX

    seed = lax.ppermute(
        value_weight,
        ("dp", "x"),
        [(z * NX + (x + 2 * (z % 2)) % NX, z * NX + x) for z in range(groups) for x in range(NX)],
    )
    owner_row = owner_map[0]
    pool = owner_row.shape[0]
    stored = locate(owner_row, history)
    pick = stored[:, None] == lax.broadcasted_iota(jnp.int32, (hist_rows, pool), 1)
    wanted = jnp.any(pick, axis=0).reshape(groups, item_rows)
    slot = jnp.cumsum(wanted.astype(jnp.int32), axis=1) - 1
    slot_pos = jnp.sum(jnp.where(pick, slot.reshape(1, pool), 0), axis=1)
    buffer_row = stored // item_rows * CAP + slot_pos
    one_hot = (
        buffer_row[:, None] == lax.broadcasted_iota(jnp.int32, (hist_rows, groups * CAP), 1)
    ).astype(jnp.bfloat16)
    grad_sums = dot(one_hot, value_grad, 0, 0).astype(jnp.bfloat16).reshape(groups, CAP, width)
    slot_ids = lax.broadcasted_iota(jnp.int32, (groups, CAP, item_rows), 1)
    asked = (wanted[:, None, :] & (slot[:, None, :] == slot_ids)).astype(jnp.bfloat16)
    asked = jnp.pad(asked, ((0, 0), (0, 0), (0, -item_rows % 128)))
    sent, seed = lax.optimization_barrier((jnp.concatenate([grad_sums, asked], axis=2), seed))
    arrived = lax.all_to_all(sent, "dp", split_axis=0, concat_axis=0, tiled=True)
    arrived = arrived.reshape(groups * CAP, -1)
    column = lax.all_gather(seed, ("y", "core"), axis=0, tiled=True)
    select = arrived[:, width : width + item_rows]

    hidden = item_hidden.astype(jnp.float32)
    item_emb, item_scale = norm_rows(hidden, item_gain)
    item_emb = item_emb.astype(jnp.bfloat16)
    outgoing = dot(select, item_emb).astype(jnp.bfloat16).reshape(groups, CAP, width)
    incoming = lax.all_to_all(outgoing, "dp", split_axis=0, concat_axis=0, tiled=True)

    mine = lax.dynamic_slice(column, (0, core * half), (block, half))
    rows = block // 2
    one_a, one_b = shift(mine[:rows], "x", 1), shift(mine[rows:], "x", 1)
    three_a, three_b = shift(mine[:rows], "x", -1), shift(mine[rows:], "x", -1)
    two_a = shift(mine[:rows], "dp", 1)
    two_b = shift(mine[rows:], "dp", -1)
    incoming, one_a, three_a, two_a, two_b = lax.optimization_barrier(
        (incoming, one_a, three_a, two_a, two_b)
    )

    total = dot(select, arrived[:, :width], 0, 0)
    high = lax.reduce_precision(total, 8, 7)
    both = jnp.concatenate([high, total - high], axis=0).astype(jnp.bfloat16)
    low_half, high_half = both[:, :half], both[:, half:]
    own = jnp.where(core == 0, low_half, high_half)
    swap = [(0, 1), (1, 0)]
    other = lax.ppermute(jnp.where(core == 0, high_half, low_half), "core", swap)
    grads = jnp.concatenate([own, other], axis=0)

    normed, _ = norm_rows(incoming.reshape(groups * CAP, width).astype(jnp.float32), user_gain)
    normed = dot(one_hot, normed.astype(jnp.bfloat16)).astype(jnp.bfloat16)
    normed = turned(normed, color * block)
    normed = jnp.concatenate([normed, lax.ppermute(normed, "core", swap)], axis=0)

    pieces = [
        (0, mine),
        (2 * block, two_a),
        (2 * block + rows, two_b),
        (block, one_a),
        (3 * block, three_a),
        (block + rows, one_b),
        (3 * block + rows, three_b),
    ]
    values = sum(dot(normed[:, at : at + p.shape[0]], p) for at, p in pieces)
    upstream = {at: dot(grads, p, 1, 1) for at, p in pieces}
    upstream = jnp.concatenate([upstream[at] for at in sorted(upstream)], axis=1)
    upstream = upstream.reshape(2, 2, item_rows, width)
    upstream = upstream[:, 0] + upstream[:, 1]
    values = values.astype(jnp.bfloat16).reshape(2, hist_rows, half)
    upstream = upstream[0] + lax.ppermute(upstream[1], "core", swap)
    theirs = lax.ppermute(values[1], "core", swap)
    values = jnp.where(
        core == 0,
        jnp.concatenate([values[0], theirs], axis=1),
        jnp.concatenate([theirs, values[0]], axis=1),
    )

    upstream = turned(upstream, (NX - color) % NX * block)
    x = item_emb.astype(jnp.float32)
    scale = lax.rsqrt(jnp.mean(x * x, axis=1, keepdims=True) + eps)
    emb_grad = norm_back(x, user_gain, scale, upstream)
    item_grad = norm_back(hidden, item_gain, item_scale, emb_grad)
    return (values, item_grad)


def solution(mesh):
    groups = mesh.shape["dp"]
    mesh = Mesh(mesh.devices.reshape(groups, NX, NY, NCORE), ("dp",) + ROW)
    everywhere = ("dp",) + ROW
    in_specs = (
        P(everywhere, None),
        P(),
        P(everywhere),
        P(ROW, None),
        P(),
        P(ROW, None),
        P(everywhere, None),
    )
    out_specs = (P(everywhere, None), P(everywhere, None))
    return jax.shard_map(local, mesh=mesh, in_specs=in_specs, out_specs=out_specs, check_vma=False)
```

```python
import itertools

import jax
import jax.numpy as jnp
from jax import lax
from jax.experimental import pallas as pl
from jax.experimental.pallas import tpu as pltpu
from jax.sharding import Mesh, PartitionSpec as P

CAP = 8
NX, NY, NCORE = 4, 8, 2
ROW = ("x", "y", "core")


eps = 1e-06


def norm_rows(values, gain):
    scale = lax.rsqrt(jnp.mean(values * values, axis=1, keepdims=True) + eps)
    return (values * scale * gain, scale)


def norm_back(values, gain, scale, upstream):
    unit = values * scale
    scaled = upstream * gain
    return scale * (scaled - unit * jnp.mean(scaled * unit, axis=1, keepdims=True))


def locate(owner_row, items):
    matches = items[:, None] == lax.broadcasted_iota(
        jnp.int32, (items.shape[0], owner_row.shape[0]), 1
    )
    return jnp.sum(jnp.where(matches, owner_row[None, :], 0), axis=1)


def dot(a, b, da=1, db=0):
    return lax.dot_general(a, b, (((da,), (db,)), ((), ())), preferred_element_type=jnp.float32)


def nt(a, b):
    return dot(a, b, 1, 1)


def turned(a, start):
    twice = jnp.concatenate([a, a], axis=1)
    return lax.dynamic_slice_in_dim(twice, start, a.shape[1], axis=1)


def route(a, axes, sizes, source):
    pairs = []
    for to in itertools.product(*[range(n) for n in sizes]):
        flat = 0
        for n, i in zip(sizes, source(*to)):
            flat = flat * n + i % n
        mine = 0
        for n, i in zip(sizes, to):
            mine = mine * n + i
        pairs.append((flat, mine))
    return lax.ppermute(a, axes, pairs)


def products(act, act_other, grads, grads_other, weight):
    rows = grads.shape[0] // 2
    forward = dot(jnp.concatenate([act, act_other], axis=0), weight)
    back = nt(jnp.concatenate([grads, grads_other], axis=0), weight)
    return (
        forward,
        back[:rows] + back[rows : 2 * rows],
        back[2 * rows : 3 * rows] + back[3 * rows :],
    )


def first_kernel(act, act_other, grads, grads_other, weight, acc, up, up_other):
    acc[...], up[...], up_other[...] = products(
        act[...], act_other[...], grads[...], grads_other[...], weight[...]
    )


def second_kernel(act, act_other, grads, grads_other, a, b, c, d, acc, up, up_other, keep, send):
    rows, width = act.shape[0], a.shape[1]
    weight = jnp.concatenate([a[...], b[...], c[...], d[...]], axis=0)
    forward, back, back_other = products(
        act[...], act_other[...], grads[...], grads_other[...], weight
    )
    items = back.shape[0]
    keep[:, :width] = acc[:rows] + forward[:rows]
    send[:, :width] = acc[rows:] + forward[rows:]
    keep[:items, width:] = up[...]
    keep[items:, width:] = back
    send[:items, width:] = up_other[...]
    send[items:, width:] = back_other


def last_kernel(place, keep, got, hidden, item_emb, item_gain, user_gain, values, item_grad, upstream):
    width = values.shape[1]
    items = hidden.shape[0]
    block = keep.shape[1] - width
    values[...] = (keep[:, :width] + got[:, :width]).astype(jnp.bfloat16)
    for step, ref in ((0, keep), (2, got)):
        for part in range(2):
            at = lax.rem(place[0] + step + part, NX) * block
            upstream[:, pl.ds(pl.multiple_of(at, block), block)] = ref[
                part * items : (part + 1) * items, width:
            ]
    x = item_emb[...].astype(jnp.float32)
    scale = lax.rsqrt(jnp.mean(x * x, axis=1, keepdims=True) + eps)
    emb_grad = norm_back(x, user_gain[...], scale, upstream[...])
    hid = hidden[...].astype(jnp.float32)
    scale = lax.rsqrt(jnp.mean(hid * hid, axis=1, keepdims=True) + eps)
    item_grad[...] = norm_back(hid, item_gain[...], scale, emb_grad)


def on_chip(kernel, shapes, *args, scratch=(), cost=None, smem=0):
    vmem = pl.BlockSpec(memory_space=pltpu.VMEM)
    return pl.pallas_call(
        kernel,
        out_shape=[jax.ShapeDtypeStruct(s, t) for s, t in shapes],
        in_specs=[pl.BlockSpec(memory_space=pltpu.SMEM)] * smem + [vmem] * (len(args) - smem),
        out_specs=[vmem] * len(shapes),
        scratch_shapes=list(scratch),
        cost_estimate=cost,
        compiler_params=pltpu.CompilerParams(vmem_limit_bytes=32 << 20),
    )(*args)


def local(item_hidden, item_gain, history, owner_map, user_gain, value_weight, value_grad):
    groups = lax.axis_size("dp")
    item_rows, width = item_hidden.shape
    hist_rows = history.shape[0]
    block = width // NX
    core = lax.axis_index("core")
    color = (lax.axis_index("x") + lax.axis_index("dp") % 2 + 2 * core) % NX
    axes, sizes = ("dp", "x", "core"), (groups, NX, NCORE)
    f32, bf16 = jnp.float32, jnp.bfloat16

    shard_a = route(value_weight, axes, sizes, lambda z, x, c: (z, x + z % 2 + 2 * c, 1 - c))
    shard_b = route(value_weight, axes, sizes, lambda z, x, c: (z, x + z % 2 + 2 * c, c))
    seed = jnp.where(
        core == 0,
        jnp.concatenate([shard_b, shard_a], axis=0),
        jnp.concatenate([shard_a, shard_b], axis=0),
    )

    owner_row = owner_map[0]
    pool = owner_row.shape[0]
    stored = locate(owner_row, history)
    pick = stored[:, None] == lax.broadcasted_iota(jnp.int32, (hist_rows, pool), 1)
    wanted = jnp.any(pick, axis=0).reshape(groups, item_rows)
    slot = jnp.cumsum(wanted.astype(jnp.int32), axis=1) - 1
    slot_pos = jnp.sum(jnp.where(pick, slot.reshape(1, pool), 0), axis=1)
    buffer_row = stored // item_rows * CAP + slot_pos
    one_hot = (
        buffer_row[:, None] == lax.broadcasted_iota(jnp.int32, (hist_rows, groups * CAP), 1)
    ).astype(bf16)
    grad_sums = dot(one_hot, value_grad, 0, 0).astype(bf16).reshape(groups, CAP, width)
    slot_ids = lax.broadcasted_iota(jnp.int32, (groups, CAP, item_rows), 1)
    asked = (wanted[:, None, :] & (slot[:, None, :] == slot_ids)).astype(bf16)
    asked = jnp.pad(asked, ((0, 0), (0, 0), (0, -item_rows % 128)))
    sent, seed = lax.optimization_barrier((jnp.concatenate([grad_sums, asked], axis=2), seed))
    arrived = lax.all_to_all(sent, "dp", split_axis=0, concat_axis=0, tiled=True)
    arrived = arrived.reshape(groups * CAP, -1)
    mine = lax.all_gather(seed, "y", axis=0, tiled=True)
    select = arrived[:, width : width + item_rows]

    item_emb, _ = norm_rows(item_hidden.astype(f32), item_gain)
    item_emb = item_emb.astype(bf16)
    outgoing = dot(select, item_emb).astype(bf16).reshape(groups, CAP, width)
    incoming = lax.all_to_all(outgoing, "dp", split_axis=0, concat_axis=0, tiled=True)

    quarter = block // 4
    cuts = [mine[i * quarter : (i + 1) * quarter] for i in range(4)]
    cross = lambda z, c: 1 - c if z % 2 else c
    pieces = [
        route(cuts[0], axes, sizes, lambda z, x, c: (z, x + 1, c)),
        route(cuts[1], axes, sizes, lambda z, x, c: (z, x - 1, 1 - c)),
        route(cuts[2], axes, sizes, lambda z, x, c: (z + 1, x, cross(z, c))),
        route(cuts[3], axes, sizes, lambda z, x, c: (z - 1, x, cross(z, c))),
    ]

    incoming, pieces[0] = lax.optimization_barrier((incoming, pieces[0]))

    swap = [(0, 1), (1, 0)]
    total = dot(select, arrived[:, :width], 0, 0)
    high = lax.reduce_precision(total, 8, 7)
    grads = jnp.concatenate([high, total - high], axis=0).astype(bf16)
    grads_other = lax.ppermute(grads, "core", swap)
    normed, _ = norm_rows(incoming.reshape(groups * CAP, width).astype(f32), user_gain)
    normed = dot(one_hot, normed.astype(bf16)).astype(bf16)
    normed = turned(normed, color * block)
    act = normed[:, : 2 * block]
    act_other = lax.ppermute(normed[:, 2 * block :], "core", swap)

    both = 2 * hist_rows
    cost = pl.CostEstimate(flops=0, bytes_accessed=0, transcendentals=0)
    acc, up, up_other = on_chip(
        first_kernel,
        [((both, width), f32), ((item_rows, block), f32), ((item_rows, block), f32)],
        act[:, :block], act_other[:, :block], grads, grads_other, mine,
        cost=cost,
    )
    keep, send = on_chip(
        second_kernel,
        [((hist_rows, width + block), f32)] * 2,
        act[:, block:], act_other[:, block:], grads, grads_other, *pieces, acc, up, up_other,
        cost=cost,
    )
    got = lax.ppermute(send, "core", swap)
    values, item_grad = on_chip(
        last_kernel,
        [((hist_rows, width), bf16), ((item_rows, width), f32)],
        color.reshape(1).astype(jnp.int32), keep, got, item_hidden, item_emb,
        item_gain.reshape(1, width), user_gain.reshape(1, width),
        scratch=[pltpu.VMEM((item_rows, width), f32)],
        smem=1,
    )
    return (values, item_grad)


def solution(mesh):
    groups = mesh.shape["dp"]
    mesh = Mesh(mesh.devices.reshape(groups, NX, NY, NCORE), ("dp",) + ROW)
    everywhere = ("dp",) + ROW
    in_specs = (
        P(everywhere, None),
        P(),
        P(everywhere),
        P(ROW, None),
        P(),
        P(ROW, None),
        P(everywhere, None),
    )
    out_specs = (P(everywhere, None), P(everywhere, None))
    return jax.shard_map(local, mesh=mesh, in_specs=in_specs, out_specs=out_specs, check_vma=False)
```

```python
import jax
import jax.numpy as jnp
from jax import lax
from jax.experimental import pallas as pl
from jax.experimental.pallas import tpu as pltpu
from jax.sharding import Mesh, PartitionSpec as P

CAP = 8
NX, NY, NCORE = 4, 8, 2
ROW = ("x", "y", "core")


eps = 1e-06


def norm_rows(values, gain):
    scale = lax.rsqrt(jnp.mean(values * values, axis=1, keepdims=True) + eps)
    return (values * scale * gain, scale)


def norm_back(values, gain, scale, upstream):
    unit = values * scale
    scaled = upstream * gain
    return scale * (scaled - unit * jnp.mean(scaled * unit, axis=1, keepdims=True))


def locate(owner_row, items):
    matches = items[:, None] == lax.broadcasted_iota(
        jnp.int32, (items.shape[0], owner_row.shape[0]), 1
    )
    return jnp.sum(jnp.where(matches, owner_row[None, :], 0), axis=1)


def dot(a, b, da=1, db=0):
    return lax.dot_general(a, b, (((da,), (db,)), ((), ())), preferred_element_type=jnp.float32)


def split(a):
    part = a.shape[1] // (NX * NY * NCORE)
    a = a.reshape(a.shape[0], NX, NY, NCORE, part).transpose(0, 3, 2, 1, 4)
    return a.reshape(a.shape[0], -1)


def products(act, act_other, grads, grads_other, weight, acc, up, up_other):
    forward = dot(jnp.concatenate([act[...], act_other[...]], axis=0), weight[...])
    back = dot(jnp.concatenate([grads[...], grads_other[...]], axis=0), weight[...], 1, 1)

    @pl.when(pl.program_id(0) == 0)
    def _():
        acc[...] = forward

    @pl.when(pl.program_id(0) > 0)
    def _():
        acc[...] += forward

    rows = up.shape[0]
    up[...] = back[:rows] + back[rows : 2 * rows]
    up_other[...] = back[2 * rows : 3 * rows] + back[3 * rows :]


def products_kernel(act, act_other, grads, grads_other, weight, keep, send, acc, up, up_other):
    step, steps = pl.program_id(0), pl.num_programs(0)
    block, width = weight.shape
    items = up.shape[0]
    at = pl.ds(pl.multiple_of(step * block, block), block)
    products(
        act, act_other, grads, grads_other, weight, acc, up.at[:, at], up_other.at[:, at]
    )

    @pl.when(step == steps - 1)
    def _():
        rows = act.shape[0]
        half = up.shape[1] // 2
        keep[:, :width] = acc[:rows]
        send[:, :width] = acc[rows:]
        for ref, sums in ((keep, up), (send, up_other)):
            ref[:items, width:] = sums[:, :half]
            ref[items:, width:] = sums[:, half:]


def last_kernel(core, keep, got, hidden, item_emb, item_gain, user_gain, values, item_grad, up):
    width = values.shape[1]
    items = hidden.shape[0]
    block = keep.shape[1] - width
    part = width // (NX * NY * NCORE)
    tile = part * NX
    values[...] = (keep[:, :width] + got[:, :width]).astype(jnp.bfloat16)
    for side, ref in ((core[0], keep), (1 - core[0], got)):
        for piece in range(2):
            at = pl.multiple_of((2 * side + piece) * block, block)
            up[:, pl.ds(at, block)] = ref[piece * items : (piece + 1) * items, width:]
    x = item_emb[...].astype(jnp.float32)
    scale = lax.rsqrt(jnp.mean(x * x, axis=1, keepdims=True) + eps)
    emb_grad = norm_back(x, user_gain[...], scale, up[...])
    hid = hidden[...].astype(jnp.float32)
    scale = lax.rsqrt(jnp.mean(hid * hid, axis=1, keepdims=True) + eps)
    up[...] = norm_back(hid, item_gain[...], scale, emb_grad)
    group = lax.broadcasted_iota(jnp.int32, (items, tile), 1) // part
    for out in range(width // tile):
        at_x, y = out // (NY // 2), 2 * (out % (NY // 2))
        total = None
        for to, (side, at_y) in enumerate(((0, y), (1, y), (0, y + 1), (1, y + 1))):
            piece = up[:, (side * NY + at_y) * tile : (side * NY + at_y + 1) * tile]
            piece = pltpu.roll(piece, (to - at_x) % NX * part, 1)
            total = piece if total is None else jnp.where(group == to, piece, total)
        item_grad[:, out * tile : (out + 1) * tile] = total


def local(item_hidden, item_gain, history, owner_map, user_gain, value_weight, value_grad):
    groups = lax.axis_size("dp")
    item_rows, width = item_hidden.shape
    hist_rows = history.shape[0]
    shard = value_weight.shape[0]
    half = width // 2
    core = lax.axis_index("core")
    f32, bf16 = jnp.float32, jnp.bfloat16

    near = [value_weight]
    for step in range(1, NX):
        pairs = [((x + step) % NX, x) for x in range(NX)]
        near.append(lax.ppermute(value_weight, "x", pairs))
    seed = lax.dynamic_slice_in_dim(
        jnp.concatenate(near + near, axis=0),
        (NX - lax.axis_index("x")) % NX * shard,
        NX * shard,
        axis=0,
    )

    owner_row = owner_map[0]
    pool = owner_row.shape[0]
    stored = locate(owner_row, history)
    pick = stored[:, None] == lax.broadcasted_iota(jnp.int32, (hist_rows, pool), 1)
    wanted = jnp.any(pick, axis=0).reshape(groups, item_rows)
    slot = jnp.cumsum(wanted.astype(jnp.int32), axis=1) - 1
    slot_pos = jnp.sum(jnp.where(pick, slot.reshape(1, pool), 0), axis=1)
    buffer_row = stored // item_rows * CAP + slot_pos
    one_hot = (
        buffer_row[:, None] == lax.broadcasted_iota(jnp.int32, (hist_rows, groups * CAP), 1)
    ).astype(bf16)
    grad_sums = dot(one_hot, value_grad, 0, 0).astype(bf16).reshape(groups, CAP, width)
    slot_ids = lax.broadcasted_iota(jnp.int32, (groups, CAP, item_rows), 1)
    asked = (wanted[:, None, :] & (slot[:, None, :] == slot_ids)).astype(bf16)
    asked = jnp.pad(asked, ((0, 0), (0, 0), (0, -item_rows % 128)))
    sent, seed = lax.optimization_barrier((jnp.concatenate([grad_sums, asked], axis=2), seed))
    weight = lax.all_gather(seed, "y", axis=0, tiled=True)
    arrived = lax.all_to_all(sent, "dp", split_axis=0, concat_axis=0, tiled=True)
    arrived = arrived.reshape(groups * CAP, -1)
    select = arrived[:, width : width + item_rows]

    hidden = split(item_hidden)
    item_gain, user_gain = split(item_gain.reshape(1, width)), split(user_gain.reshape(1, width))
    item_emb, _ = norm_rows(hidden.astype(f32), item_gain)
    item_emb = item_emb.astype(bf16)
    outgoing = dot(select, item_emb).astype(bf16).reshape(groups, CAP, width)
    incoming = lax.all_to_all(outgoing, "dp", split_axis=0, concat_axis=0, tiled=True)

    swap = [(0, 1), (1, 0)]
    total = dot(select, arrived[:, :width], 0, 0)
    high = lax.reduce_precision(total, 8, 7)
    grads = jnp.concatenate([high, total - high], axis=0).astype(bf16)
    grads_other = lax.ppermute(grads, "core", swap)
    normed, _ = norm_rows(incoming.reshape(groups * CAP, width).astype(f32), user_gain)
    normed = dot(one_hot, normed.astype(bf16)).astype(bf16)
    low, high = normed[:, :half], normed[:, half:]
    act = jnp.where(core == 0, low, high)
    act_other = lax.ppermute(jnp.where(core == 0, high, low), "core", swap)

    steps = 4
    block = half // steps
    piece = pl.BlockSpec((hist_rows, block), lambda i: (0, i))
    once = pl.BlockSpec((2 * item_rows, width), lambda i: (0, 0))
    result = jax.ShapeDtypeStruct((hist_rows, width + half * item_rows // hist_rows), f32)
    keep, send = pl.pallas_call(
        products_kernel,
        grid=(steps,),
        out_shape=[result, result],
        in_specs=[piece, piece, once, once, pl.BlockSpec((block, width), lambda i: (i, 0))],
        out_specs=[pl.BlockSpec(result.shape, lambda i: (0, 0))] * 2,
        scratch_shapes=[
            pltpu.VMEM((2 * hist_rows, width), f32),
            pltpu.VMEM((item_rows, half), f32),
            pltpu.VMEM((item_rows, half), f32),
        ],
        cost_estimate=pl.CostEstimate(
            flops=8 * hist_rows * half * width, bytes_accessed=10 << 20, transcendentals=0
        ),
        compiler_params=pltpu.CompilerParams(vmem_limit_bytes=32 << 20),
    )(act, act_other, grads, grads_other, weight)
    got = lax.ppermute(send, "core", swap)

    vmem = pl.BlockSpec(memory_space=pltpu.VMEM)
    values, item_grad = pl.pallas_call(
        last_kernel,
        out_shape=[
            jax.ShapeDtypeStruct((hist_rows, width), bf16),
            jax.ShapeDtypeStruct((item_rows, width), f32),
        ],
        in_specs=[pl.BlockSpec(memory_space=pltpu.SMEM)] + [vmem] * 6,
        out_specs=[vmem] * 2,
        scratch_shapes=[pltpu.VMEM((item_rows, width), f32)],
        compiler_params=pltpu.CompilerParams(vmem_limit_bytes=32 << 20),
    )(core.reshape(1).astype(jnp.int32), keep, got, hidden, item_emb, item_gain, user_gain)
    return (values, item_grad)


def solution(mesh):
    groups = mesh.shape["dp"]
    mesh = Mesh(mesh.devices.reshape(groups, NX, NY, NCORE), ("dp",) + ROW)
    everywhere = ("dp",) + ROW
    in_specs = (
        P(everywhere, None),
        P(),
        P(everywhere),
        P(ROW, None),
        P(),
        P(ROW, None),
        P(everywhere, None),
    )
    out_specs = (P(everywhere, None), P(everywhere, None))
    return jax.shard_map(local, mesh=mesh, in_specs=in_specs, out_specs=out_specs, check_vma=False)
```

```python
import jax
import jax.numpy as jnp
from jax import lax
from jax.experimental import pallas as pl
from jax.experimental.pallas import tpu as pltpu
from jax.sharding import Mesh, PartitionSpec as P

CAP = 8
NX, NY, NCORE = 4, 8, 2
ROW = ("x", "y", "core")


eps = 1e-06


def norm_rows(values, gain):
    scale = lax.rsqrt(jnp.mean(values * values, axis=1, keepdims=True) + eps)
    return (values * scale * gain, scale)


def norm_back(values, gain, scale, upstream):
    unit = values * scale
    scaled = upstream * gain
    return scale * (scaled - unit * jnp.mean(scaled * unit, axis=1, keepdims=True))


def locate(owner_row, items):
    matches = items[:, None] == lax.broadcasted_iota(
        jnp.int32, (items.shape[0], owner_row.shape[1]), 1
    )
    return jnp.sum(jnp.where(matches, owner_row, 0), axis=1)


def dot(a, b, da=1, db=0):
    return lax.dot_general(a, b, (((da,), (db,)), ((), ())), preferred_element_type=jnp.float32)


def split(a):
    part = a.shape[1] // (NX * NY * NCORE)
    a = a.reshape(a.shape[0], NX, NY, NCORE, part).transpose(0, 3, 2, 1, 4)
    return a.reshape(a.shape[0], -1)


def products_kernel(act, act_other, grads, grads_other, weight, keep, send, held, sems):
    parts = sems.shape[0]
    block = held.shape[0] // parts
    cuts = [slice(i * block, (i + 1) * block) for i in range(parts)]
    copies = [
        pltpu.make_async_copy(weight.at[cut], held.at[cut], sems.at[i])
        for i, cut in enumerate(cuts)
    ]
    for copy in copies:
        copy.start()
    rows, half = act.shape
    width = held.shape[1]
    items = grads.shape[0] // 2
    both = jnp.concatenate([grads[...], grads_other[...]], axis=0)
    for i, (copy, cut) in enumerate(zip(copies, cuts)):
        copy.wait()
        back = dot(both, held[cut], 1, 1)
        row, column = divmod(i * block, half // 2)
        row = row * items
        at = slice(width + column, width + column + block)
        keep[row : row + items, at] = back[:items] + back[items : 2 * items]
        send[row : row + items, at] = back[2 * items : 3 * items] + back[3 * items :]
    both = jnp.concatenate([act[...], act_other[...]], axis=0)
    for i in range(parts):
        at = slice(i * width // parts, (i + 1) * width // parts)
        forward = dot(both, held[:, at])
        keep[:, at] = forward[:rows]
        send[:, at] = forward[rows:]


def last_kernel(core, keep, got, hidden, item_emb, item_gain, user_gain, values, item_grad, up):
    width = values.shape[1]
    items = hidden.shape[0]
    block = keep.shape[1] - width
    part = width // (NX * NY * NCORE)
    tile = part * NX
    values[...] = (keep[:, :width] + got[:, :width]).astype(jnp.bfloat16)
    for side, ref in ((core[0], keep), (1 - core[0], got)):
        for piece in range(2):
            at = pl.multiple_of((2 * side + piece) * block, block)
            up[:, pl.ds(at, block)] = ref[piece * items : (piece + 1) * items, width:]
    x = item_emb[...].astype(jnp.float32)
    scale = lax.rsqrt(jnp.mean(x * x, axis=1, keepdims=True) + eps)
    emb_grad = norm_back(x, user_gain[...], scale, up[...])
    hid = hidden[...].astype(jnp.float32)
    scale = lax.rsqrt(jnp.mean(hid * hid, axis=1, keepdims=True) + eps)
    up[...] = norm_back(hid, item_gain[...], scale, emb_grad)
    group = lax.broadcasted_iota(jnp.int32, (items, tile), 1) // part
    for out in range(width // tile):
        at_x, y = out // (NY // 2), 2 * (out % (NY // 2))
        total = None
        for to, (side, at_y) in enumerate(((0, y), (1, y), (0, y + 1), (1, y + 1))):
            piece = up[:, (side * NY + at_y) * tile : (side * NY + at_y + 1) * tile]
            piece = pltpu.roll(piece, (to - at_x) % NX * part, 1)
            total = piece if total is None else jnp.where(group == to, piece, total)
        item_grad[:, out * tile : (out + 1) * tile] = total


def local(item_hidden, item_gain, history, owner_map, user_gain, value_weight, value_grad):
    groups = lax.axis_size("dp")
    item_rows, width = item_hidden.shape
    hist_rows = history.shape[0]
    half = width // 2
    core = lax.axis_index("core")
    f32, bf16 = jnp.float32, jnp.bfloat16

    seed = lax.all_gather(value_weight, "x", axis=0, tiled=True)
    history, seed = lax.optimization_barrier((history, seed))
    weight = lax.all_gather(seed, "y", axis=0, tiled=True)

    pool = owner_map.shape[1]
    stored = locate(owner_map, history)
    pick = stored[:, None] == lax.broadcasted_iota(jnp.int32, (hist_rows, pool), 1)
    wanted = jnp.any(pick, axis=0).reshape(groups, item_rows)
    slot = jnp.cumsum(wanted.astype(jnp.int32), axis=1) - 1
    slot_pos = jnp.sum(jnp.where(pick, slot.reshape(1, pool), 0), axis=1)
    buffer_row = stored // item_rows * CAP + slot_pos
    one_hot = (
        buffer_row[:, None] == lax.broadcasted_iota(jnp.int32, (hist_rows, groups * CAP), 1)
    ).astype(bf16)
    grad_sums = dot(one_hot, value_grad, 0, 0).astype(bf16).reshape(groups, CAP, width)
    slot_ids = lax.broadcasted_iota(jnp.int32, (groups, CAP, item_rows), 1)
    asked = (wanted[:, None, :] & (slot[:, None, :] == slot_ids)).astype(bf16)
    asked = jnp.pad(asked, ((0, 0), (0, 0), (0, -item_rows % 128)))
    sent = jnp.concatenate([grad_sums, asked], axis=2)
    arrived = lax.all_to_all(sent, "dp", split_axis=0, concat_axis=0, tiled=True)
    arrived = arrived.reshape(groups * CAP, -1)
    select = arrived[:, width : width + item_rows]

    hidden = split(item_hidden)
    item_gain, user_gain = split(item_gain.reshape(1, width)), split(user_gain.reshape(1, width))
    item_emb, _ = norm_rows(hidden.astype(f32), item_gain)
    item_emb = item_emb.astype(bf16)
    outgoing = dot(select, item_emb).astype(bf16).reshape(groups, CAP, width)
    incoming = lax.all_to_all(outgoing, "dp", split_axis=0, concat_axis=0, tiled=True)

    swap = [(0, 1), (1, 0)]
    total = dot(select, arrived[:, :width], 0, 0)
    high = lax.reduce_precision(total, 8, 7)
    grads = jnp.concatenate([high, total - high], axis=0).astype(bf16)
    grads_other = lax.ppermute(grads, "core", swap)
    normed, _ = norm_rows(incoming.reshape(groups * CAP, width).astype(f32), user_gain)
    normed = dot(one_hot, normed.astype(bf16)).astype(bf16)
    low, high = normed[:, :half], normed[:, half:]
    act = jnp.where(core == 0, low, high)
    act_other = lax.ppermute(jnp.where(core == 0, high, low), "core", swap)

    vmem = pl.BlockSpec(memory_space=pltpu.VMEM)
    result = jax.ShapeDtypeStruct((hist_rows, width + half * item_rows // hist_rows), f32)
    keep, send = pl.pallas_call(
        products_kernel,
        out_shape=[result, result],
        in_specs=[vmem] * 4 + [pl.BlockSpec(memory_space=pltpu.HBM)],
        out_specs=[vmem] * 2,
        scratch_shapes=[pltpu.VMEM((half, width), bf16), pltpu.SemaphoreType.DMA((4,))],
        cost_estimate=pl.CostEstimate(
            flops=8 * hist_rows * half * width, bytes_accessed=10 << 20, transcendentals=0
        ),
        compiler_params=pltpu.CompilerParams(vmem_limit_bytes=52 << 20),
    )(act, act_other, grads, grads_other, weight)
    got = lax.ppermute(send, "core", swap)
    values, item_grad = pl.pallas_call(
        last_kernel,
        out_shape=[
            jax.ShapeDtypeStruct((hist_rows, width), bf16),
            jax.ShapeDtypeStruct((item_rows, width), f32),
        ],
        in_specs=[pl.BlockSpec(memory_space=pltpu.SMEM)] + [vmem] * 6,
        out_specs=[vmem] * 2,
        scratch_shapes=[pltpu.VMEM((item_rows, width), f32)],
        compiler_params=pltpu.CompilerParams(vmem_limit_bytes=12 << 20),
    )(core.reshape(1).astype(jnp.int32), keep, got, hidden, item_emb, item_gain, user_gain)
    return (values, item_grad)


def solution(mesh):
    groups = mesh.shape["dp"]
    mesh = Mesh(mesh.devices.reshape(groups, NX, NY, NCORE), ("dp",) + ROW)
    everywhere = ("dp",) + ROW
    in_specs = (
        P(everywhere, None),
        P(),
        P(everywhere),
        P(ROW, None),
        P(),
        P(ROW, None),
        P(everywhere, None),
    )
    out_specs = (P(everywhere, None), P(everywhere, None))
    return jax.shard_map(local, mesh=mesh, in_specs=in_specs, out_specs=out_specs, check_vma=False)
```

```python
import jax
import jax.numpy as jnp
from jax import lax
from jax.experimental import pallas as pl
from jax.experimental.pallas import tpu as pltpu
from jax.sharding import Mesh, PartitionSpec as P

CAP = 8
NX, NY, NCORE = 4, 8, 2
ROW = ("x", "y", "core")


eps = 1e-06


def norm_rows(values, gain):
    scale = lax.rsqrt(jnp.mean(values * values, axis=1, keepdims=True) + eps)
    return (values * scale * gain, scale)


def norm_back(values, gain, scale, upstream):
    unit = values * scale
    scaled = upstream * gain
    return scale * (scaled - unit * jnp.mean(scaled * unit, axis=1, keepdims=True))


def locate(owner_row, items):
    matches = items[:, None] == lax.broadcasted_iota(
        jnp.int32, (items.shape[0], owner_row.shape[1]), 1
    )
    return jnp.sum(jnp.where(matches, owner_row, 0), axis=1)


def dot(a, b, da=1, db=0):
    return lax.dot_general(a, b, (((da,), (db,)), ((), ())), preferred_element_type=jnp.float32)


def split(a):
    part = a.shape[1] // (NX * NY * NCORE)
    a = a.reshape(a.shape[0], NX, NY, NCORE, part).transpose(0, 3, 2, 1, 4)
    return a.reshape(a.shape[0], -1)


def fetch(weight, held, sems):
    parts = sems.shape[0]
    block = held.shape[0] // parts
    cuts = [slice(i * block, (i + 1) * block) for i in range(parts)]
    copies = [
        pltpu.make_async_copy(weight.at[cut], held.at[cut], sems.at[i])
        for i, cut in enumerate(cuts)
    ]
    for copy in copies:
        copy.start()
    return cuts, copies


def sent_kernel(act_other, grads, grads_other, weight, up, send, held, ready, sems, out_sems):
    cuts, copies = fetch(weight, held, sems)
    half, width = held.shape
    items = grads.shape[0] // 2
    both = jnp.concatenate([grads[...], grads_other[...]], axis=0)
    for cut, copy in zip(cuts, copies):
        copy.wait()
        back = dot(both, held[cut], 1, 1)
        row, column = divmod(cut.start, half // 2)
        row, to = row * items, slice(column, column + cut.stop - cut.start)
        up[row : row + items, to] = back[:items] + back[items : 2 * items]
        to = slice(width + to.start, width + to.stop)
        ready[row : row + items, to] = back[2 * items : 3 * items] + back[3 * items :]
    parts = len(cuts)
    ends = [i * width // parts for i in range(parts + 1)] + [send.shape[1]]
    outs = [
        pltpu.make_async_copy(ready.at[:, lo:hi], send.at[:, lo:hi], out_sems.at[i])
        for i, (lo, hi) in enumerate(zip(ends[:-1], ends[1:]))
    ]
    outs[-1].start()
    for i in range(parts):
        at = slice(ends[i], ends[i + 1])
        ready[:, at] = dot(act_other[...], held[:, at])
        outs[i].start()
    for out in outs:
        out.wait()


def kept_kernel(act, weight, keep, held, sems):
    cuts, copies = fetch(weight, held, sems)
    total = None
    for cut, copy in zip(cuts, copies):
        copy.wait()
        part = dot(act[:, cut], held[cut])
        total = part if total is None else total + part
    keep[...] = total


def last_kernel(core, keep, sums, got, hidden, item_emb, item_gain, user_gain, values, item_grad, up):
    width = values.shape[1]
    items = hidden.shape[0]
    block = sums.shape[1]
    part = width // (NX * NY * NCORE)
    tile = part * NX
    values[...] = (keep[...] + got[:, :width]).astype(jnp.bfloat16)
    for side, ref, skip in ((core[0], sums, 0), (1 - core[0], got, width)):
        for piece in range(2):
            at = pl.multiple_of((2 * side + piece) * block, block)
            up[:, pl.ds(at, block)] = ref[piece * items : (piece + 1) * items, skip:]
    x = item_emb[...].astype(jnp.float32)
    scale = lax.rsqrt(jnp.mean(x * x, axis=1, keepdims=True) + eps)
    emb_grad = norm_back(x, user_gain[...], scale, up[...])
    hid = hidden[...].astype(jnp.float32)
    scale = lax.rsqrt(jnp.mean(hid * hid, axis=1, keepdims=True) + eps)
    up[...] = norm_back(hid, item_gain[...], scale, emb_grad)
    group = lax.broadcasted_iota(jnp.int32, (items, tile), 1) // part
    for out in range(width // tile):
        at_x, y = out // (NY // 2), 2 * (out % (NY // 2))
        total = None
        for to, (side, at_y) in enumerate(((0, y), (1, y), (0, y + 1), (1, y + 1))):
            piece = up[:, (side * NY + at_y) * tile : (side * NY + at_y + 1) * tile]
            piece = pltpu.roll(piece, (to - at_x) % NX * part, 1)
            total = piece if total is None else jnp.where(group == to, piece, total)
        item_grad[:, out * tile : (out + 1) * tile] = total


def local(item_hidden, item_gain, history, owner_map, user_gain, value_weight, value_grad):
    groups = lax.axis_size("dp")
    item_rows, width = item_hidden.shape
    hist_rows = history.shape[0]
    half = width // 2
    core = lax.axis_index("core")
    f32, bf16 = jnp.float32, jnp.bfloat16

    seed = lax.all_gather(value_weight, "x", axis=0, tiled=True)
    history, seed = lax.optimization_barrier((history, seed))
    weight = lax.all_gather(seed, "y", axis=0, tiled=True)

    pool = owner_map.shape[1]
    stored = locate(owner_map, history)
    pick = stored[:, None] == lax.broadcasted_iota(jnp.int32, (hist_rows, pool), 1)
    wanted = jnp.any(pick, axis=0).reshape(groups, item_rows)
    slot = jnp.cumsum(wanted.astype(jnp.int32), axis=1) - 1
    slot_pos = jnp.sum(jnp.where(pick, slot.reshape(1, pool), 0), axis=1)
    buffer_row = stored // item_rows * CAP + slot_pos
    one_hot = (
        buffer_row[:, None] == lax.broadcasted_iota(jnp.int32, (hist_rows, groups * CAP), 1)
    ).astype(bf16)
    grad_sums = dot(one_hot, value_grad, 0, 0).astype(bf16).reshape(groups, CAP, width)
    slot_ids = lax.broadcasted_iota(jnp.int32, (groups, CAP, item_rows), 1)
    asked = (wanted[:, None, :] & (slot[:, None, :] == slot_ids)).astype(bf16)
    asked = jnp.pad(asked, ((0, 0), (0, 0), (0, -item_rows % 128)))
    sent = jnp.concatenate([grad_sums, asked], axis=2)
    arrived = lax.all_to_all(sent, "dp", split_axis=0, concat_axis=0, tiled=True)
    arrived = arrived.reshape(groups * CAP, -1)
    select = arrived[:, width : width + item_rows]

    hidden = split(item_hidden)
    item_gain, user_gain = split(item_gain.reshape(1, width)), split(user_gain.reshape(1, width))
    item_emb, _ = norm_rows(hidden.astype(f32), item_gain)
    item_emb = item_emb.astype(bf16)
    outgoing = dot(select, item_emb).astype(bf16).reshape(groups, CAP, width)
    incoming = lax.all_to_all(outgoing, "dp", split_axis=0, concat_axis=0, tiled=True)

    swap = [(0, 1), (1, 0)]
    total = dot(select, arrived[:, :width], 0, 0)
    high = lax.reduce_precision(total, 8, 7)
    grads = jnp.concatenate([high, total - high], axis=0).astype(bf16)
    grads_other = lax.ppermute(grads, "core", swap)
    normed, _ = norm_rows(incoming.reshape(groups * CAP, width).astype(f32), user_gain)
    normed = dot(one_hot, normed.astype(bf16)).astype(bf16)
    low, high = normed[:, :half], normed[:, half:]
    act = jnp.where(core == 0, low, high)
    act_other = lax.ppermute(jnp.where(core == 0, high, low), "core", swap)

    vmem = pl.BlockSpec(memory_space=pltpu.VMEM)
    hbm = pl.BlockSpec(memory_space=pltpu.HBM)
    extra = half * item_rows // hist_rows
    held = [pltpu.VMEM((half, width), bf16)]
    flops = 2 * hist_rows * half * width
    sums, send = pl.pallas_call(
        sent_kernel,
        out_shape=[
            jax.ShapeDtypeStruct((hist_rows, extra), f32),
            jax.ShapeDtypeStruct((hist_rows, width + extra), f32),
        ],
        in_specs=[vmem] * 3 + [hbm],
        out_specs=[vmem, hbm],
        scratch_shapes=held
        + [
            pltpu.VMEM((hist_rows, width + extra), f32),
            pltpu.SemaphoreType.DMA((4,)),
            pltpu.SemaphoreType.DMA((5,)),
        ],
        cost_estimate=pl.CostEstimate(flops=3 * flops, bytes_accessed=6 << 20, transcendentals=0),
        compiler_params=pltpu.CompilerParams(vmem_limit_bytes=52 << 20),
    )(act_other, grads, grads_other, weight)
    got = lax.ppermute(send, "core", swap)
    (keep,) = pl.pallas_call(
        kept_kernel,
        out_shape=[jax.ShapeDtypeStruct((hist_rows, width), f32)],
        in_specs=[vmem, hbm],
        out_specs=[vmem],
        scratch_shapes=held + [pltpu.SemaphoreType.DMA((4,))],
        cost_estimate=pl.CostEstimate(flops=flops, bytes_accessed=5 << 20, transcendentals=0),
        compiler_params=pltpu.CompilerParams(vmem_limit_bytes=52 << 20),
    )(act, weight)
    values, item_grad = pl.pallas_call(
        last_kernel,
        out_shape=[
            jax.ShapeDtypeStruct((hist_rows, width), bf16),
            jax.ShapeDtypeStruct((item_rows, width), f32),
        ],
        in_specs=[pl.BlockSpec(memory_space=pltpu.SMEM)] + [vmem] * 7,
        out_specs=[vmem] * 2,
        scratch_shapes=[pltpu.VMEM((item_rows, width), f32)],
        compiler_params=pltpu.CompilerParams(vmem_limit_bytes=12 << 20),
    )(core.reshape(1).astype(jnp.int32), keep, sums, got, hidden, item_emb, item_gain, user_gain)
    return (values, item_grad)


def solution(mesh):
    groups = mesh.shape["dp"]
    mesh = Mesh(mesh.devices.reshape(groups, NX, NY, NCORE), ("dp",) + ROW)
    everywhere = ("dp",) + ROW
    in_specs = (
        P(everywhere, None),
        P(),
        P(everywhere),
        P(ROW, None),
        P(),
        P(ROW, None),
        P(everywhere, None),
    )
    out_specs = (P(everywhere, None), P(everywhere, None))
    return jax.shard_map(local, mesh=mesh, in_specs=in_specs, out_specs=out_specs, check_vma=False)
```

```python
import jax
import jax.numpy as jnp
from jax import lax
from jax.experimental import pallas as pl
from jax.experimental.pallas import tpu as pltpu
from jax.sharding import Mesh, PartitionSpec as P

CAP = 8
NX, NY, NCORE = 4, 8, 2
ROW = ("x", "y", "core")


eps = 1e-06


def norm_rows(values, gain):
    scale = lax.rsqrt(jnp.mean(values * values, axis=1, keepdims=True) + eps)
    return (values * scale * gain, scale)


def norm_back(values, gain, scale, upstream):
    unit = values * scale
    scaled = upstream * gain
    return scale * (scaled - unit * jnp.mean(scaled * unit, axis=1, keepdims=True))


def locate(owner_row, items):
    matches = items[:, None] == lax.broadcasted_iota(
        jnp.int32, (items.shape[0], owner_row.shape[1]), 1
    )
    return jnp.sum(jnp.where(matches, owner_row, 0), axis=1)


def dot(a, b, da=1, db=0):
    return lax.dot_general(a, b, (((da,), (db,)), ((), ())), preferred_element_type=jnp.float32)


def split(a):
    part = a.shape[1] // (NX * NY * NCORE)
    a = a.reshape(a.shape[0], NX, NY, NCORE, part).transpose(0, 3, 2, 1, 4)
    return a.reshape(a.shape[0], -1)


def lanes(place, width):
    return pl.ds(pl.multiple_of(place * width, width), width)


def pick_lanes(act, places, width):
    return jnp.concatenate([act[:, lanes(p, width)] for p in places], axis=1)


def back_products(grads, grads_other, blocks, places, up, up_other):
    items = grads.shape[0] // 2
    both = jnp.concatenate([grads[...], grads_other[...]], axis=0)
    weight = jnp.concatenate([b[...] for b in blocks], axis=0)
    back = dot(both, weight, 1, 1)
    width = weight.shape[0] // len(places)
    per_row = NY // 2
    for i, place in enumerate(places):
        part = back[:, i * width : (i + 1) * width]
        rows = pl.ds(pl.multiple_of(lax.div(place, per_row) * items, items), items)
        at = lanes(lax.rem(place, per_row), width)
        up[rows, at] = part[:items] + part[items : 2 * items]
        up_other[rows, at] = part[2 * items : 3 * items] + part[3 * items :]


def early_kernel(y, act, act_other, grads, grads_other, *refs):
    blocks, (acc, acc_other, up, up_other) = refs[:5], refs[5:]
    places = [lax.rem(y[0] + step, NY) for step in (0, 1, NY - 1, 2, NY - 2)]
    up[...] = jnp.zeros_like(up)
    up_other[...] = jnp.zeros_like(up_other)
    back_products(grads, grads_other, blocks, places, up, up_other)
    rows, width = acc.shape
    block = blocks[0].shape[0]
    both = jnp.concatenate(
        [pick_lanes(act, places, block), pick_lanes(act_other, places, block)], axis=0
    )
    for lo in range(0, width, 512):
        at = slice(lo, lo + 512)
        forward = dot(both, jnp.concatenate([b[:, at] for b in blocks], axis=0))
        acc[:, at] = forward[:rows]
        acc_other[:, at] = forward[rows:]


def late_places(y):
    return [lax.rem(y[0] + step, NY) for step in (3, NY - 3, 4)]


def sent_kernel(y, act_other, grads, grads_other, acc_other, up_early, up_other_early, *refs):
    blocks, (up, send, sums) = refs[:4], refs[4:]
    places = late_places(y)
    up[...] = up_early[...]
    sums[...] = up_other_early[...]
    back_products(grads, grads_other, blocks, places, up, sums)
    rows, width = acc_other.shape
    send[:, width:] = sums[...]
    both = pick_lanes(act_other, places, blocks[0].shape[0])
    for lo in range(0, width, 512):
        at = slice(lo, lo + 512)
        weight = jnp.concatenate([b[:, at] for b in blocks], axis=0)
        send[:, at] = acc_other[:, at] + dot(both, weight)


def kept_kernel(y, act, acc, *refs):
    blocks, keep = refs[:4], refs[4]
    both = pick_lanes(act, late_places(y), blocks[0].shape[0])
    for lo in range(0, acc.shape[1], 512):
        at = slice(lo, lo + 512)
        weight = jnp.concatenate([b[:, at] for b in blocks], axis=0)
        keep[:, at] = acc[:, at] + dot(both, weight)


def on_chip(kernel, scalar, *args, out, scratch=(), flops=0):
    vmem = pl.BlockSpec(memory_space=pltpu.VMEM)
    return pl.pallas_call(
        kernel,
        out_shape=[jax.ShapeDtypeStruct(shape, kind) for shape, kind in out],
        in_specs=[pl.BlockSpec(memory_space=pltpu.SMEM)] + [vmem] * len(args),
        out_specs=[vmem] * len(out),
        scratch_shapes=list(scratch),
        cost_estimate=pl.CostEstimate(flops=flops, bytes_accessed=0, transcendentals=0),
        compiler_params=pltpu.CompilerParams(vmem_limit_bytes=16 << 20),
    )(scalar.reshape(1).astype(jnp.int32), *args)


def last_kernel(core, keep, sums, got, hidden, item_emb, item_gain, user_gain, values, item_grad, up):
    width = values.shape[1]
    items = hidden.shape[0]
    block = sums.shape[1]
    part = width // (NX * NY * NCORE)
    tile = part * NX
    values[...] = (keep[...] + got[:, :width]).astype(jnp.bfloat16)
    for side, ref, skip in ((core[0], sums, 0), (1 - core[0], got, width)):
        for piece in range(2):
            at = pl.multiple_of((2 * side + piece) * block, block)
            up[:, pl.ds(at, block)] = ref[piece * items : (piece + 1) * items, skip:]
    x = item_emb[...].astype(jnp.float32)
    scale = lax.rsqrt(jnp.mean(x * x, axis=1, keepdims=True) + eps)
    emb_grad = norm_back(x, user_gain[...], scale, up[...])
    hid = hidden[...].astype(jnp.float32)
    scale = lax.rsqrt(jnp.mean(hid * hid, axis=1, keepdims=True) + eps)
    up[...] = norm_back(hid, item_gain[...], scale, emb_grad)
    group = lax.broadcasted_iota(jnp.int32, (items, tile), 1) // part
    for out in range(width // tile):
        at_x, y = out // (NY // 2), 2 * (out % (NY // 2))
        total = None
        for to, (side, at_y) in enumerate(((0, y), (1, y), (0, y + 1), (1, y + 1))):
            piece = up[:, (side * NY + at_y) * tile : (side * NY + at_y + 1) * tile]
            piece = pltpu.roll(piece, (to - at_x) % NX * part, 1)
            total = piece if total is None else jnp.where(group == to, piece, total)
        item_grad[:, out * tile : (out + 1) * tile] = total


def local(item_hidden, item_gain, history, owner_map, user_gain, value_weight, value_grad):
    groups = lax.axis_size("dp")
    item_rows, width = item_hidden.shape
    hist_rows = history.shape[0]
    half = width // 2
    core = lax.axis_index("core")
    f32, bf16 = jnp.float32, jnp.bfloat16

    seed = lax.all_gather(value_weight, "x", axis=0, tiled=True)
    history, seed = lax.optimization_barrier((history, seed))
    around = lambda a, step: lax.ppermute(a, "y", [((i + step) % NY, i) for i in range(NY)])
    up_one, down_one = around(seed, 1), around(seed, -1)

    pool = owner_map.shape[1]
    stored = locate(owner_map, history)
    pick = stored[:, None] == lax.broadcasted_iota(jnp.int32, (hist_rows, pool), 1)
    wanted = jnp.any(pick, axis=0).reshape(groups, item_rows)
    slot = jnp.cumsum(wanted.astype(jnp.int32), axis=1) - 1
    slot_pos = jnp.sum(jnp.where(pick, slot.reshape(1, pool), 0), axis=1)
    buffer_row = stored // item_rows * CAP + slot_pos
    one_hot = (
        buffer_row[:, None] == lax.broadcasted_iota(jnp.int32, (hist_rows, groups * CAP), 1)
    ).astype(bf16)
    grad_sums = dot(one_hot, value_grad, 0, 0).astype(bf16).reshape(groups, CAP, width)
    slot_ids = lax.broadcasted_iota(jnp.int32, (groups, CAP, item_rows), 1)
    asked = (wanted[:, None, :] & (slot[:, None, :] == slot_ids)).astype(bf16)
    asked = jnp.pad(asked, ((0, 0), (0, 0), (0, -item_rows % 128)))
    sent = jnp.concatenate([grad_sums, asked], axis=2)
    arrived = lax.all_to_all(sent, "dp", split_axis=0, concat_axis=0, tiled=True)
    up_two, down_two = around(up_one, 1), around(down_one, -1)
    arrived, up_two, down_two = lax.optimization_barrier((arrived, up_two, down_two))
    arrived = arrived.reshape(groups * CAP, -1)
    select = arrived[:, width : width + item_rows]

    hidden = split(item_hidden)
    item_gain, user_gain = split(item_gain.reshape(1, width)), split(user_gain.reshape(1, width))
    item_emb, _ = norm_rows(hidden.astype(f32), item_gain)
    item_emb = item_emb.astype(bf16)
    outgoing = dot(select, item_emb).astype(bf16).reshape(groups, CAP, width)
    incoming = lax.all_to_all(outgoing, "dp", split_axis=0, concat_axis=0, tiled=True)
    up_three, down_three = around(up_two, 1), around(down_two, -1)
    incoming, up_three, down_three = lax.optimization_barrier((incoming, up_three, down_three))
    rows = seed.shape[0] // 2
    up_four, down_four = around(up_three[:rows], 1), around(down_three[rows:], -1)

    swap = [(0, 1), (1, 0)]
    total = dot(select, arrived[:, :width], 0, 0)
    high = lax.reduce_precision(total, 8, 7)
    grads = jnp.concatenate([high, total - high], axis=0).astype(bf16)
    grads_other = lax.ppermute(grads, "core", swap)
    normed, _ = norm_rows(incoming.reshape(groups * CAP, width).astype(f32), user_gain)
    normed = dot(one_hot, normed.astype(bf16)).astype(bf16)
    low, high = normed[:, :half], normed[:, half:]
    act = jnp.where(core == 0, low, high)
    act_other = lax.ppermute(jnp.where(core == 0, high, low), "core", swap)

    early = (seed, up_one, down_one, up_two, down_two)
    late = (up_three, down_three, up_four, down_four)
    y = lax.axis_index("y")
    part = ((hist_rows, half * item_rows // hist_rows), f32)
    full = ((hist_rows, width), f32)
    acc, acc_other, sums, sums_other = on_chip(
        early_kernel, y, act, act_other, grads, grads_other, *early, out=[full, full, part, part]
    )
    sums, send = on_chip(
        sent_kernel, y, act_other, grads, grads_other, acc_other, sums, sums_other, *late,
        out=[part, ((hist_rows, width + part[0][1]), f32)],
        scratch=[pltpu.VMEM(*part)],
    )
    got = lax.ppermute(send, "core", swap)
    (keep,) = on_chip(kept_kernel, y, act, acc, *late, out=[full])
    values, item_grad = on_chip(
        last_kernel, core, keep, sums, got, hidden, item_emb, item_gain, user_gain,
        out=[((hist_rows, width), bf16), ((item_rows, width), f32)],
        scratch=[pltpu.VMEM((item_rows, width), f32)],
    )
    return (values, item_grad)


def solution(mesh):
    groups = mesh.shape["dp"]
    mesh = Mesh(mesh.devices.reshape(groups, NX, NY, NCORE), ("dp",) + ROW)
    everywhere = ("dp",) + ROW
    in_specs = (
        P(everywhere, None),
        P(),
        P(everywhere),
        P(ROW, None),
        P(),
        P(ROW, None),
        P(everywhere, None),
    )
    out_specs = (P(everywhere, None), P(everywhere, None))
    return jax.shard_map(local, mesh=mesh, in_specs=in_specs, out_specs=out_specs, check_vma=False)
```

```python
import jax
import jax.numpy as jnp
from jax import lax
from jax.experimental import pallas as pl
from jax.experimental.pallas import tpu as pltpu
from jax.sharding import Mesh, PartitionSpec as P

CAP = 8
NX, NY, NCORE = 4, 8, 2
ROW = ("x", "y", "core")


eps = 1e-06


def norm_rows(values, gain):
    scale = lax.rsqrt(jnp.mean(values * values, axis=1, keepdims=True) + eps)
    return (values * scale * gain, scale)


def norm_back(values, gain, scale, upstream):
    unit = values * scale
    scaled = upstream * gain
    return scale * (scaled - unit * jnp.mean(scaled * unit, axis=1, keepdims=True))


def locate(owner_row, items):
    matches = items[:, None] == lax.broadcasted_iota(
        jnp.int32, (items.shape[0], owner_row.shape[1]), 1
    )
    return jnp.sum(jnp.where(matches, owner_row, 0), axis=1)


def dot(a, b, da=1, db=0):
    return lax.dot_general(a, b, (((da,), (db,)), ((), ())), preferred_element_type=jnp.float32)


def split(a):
    part = a.shape[1] // (NX * NY * NCORE)
    a = a.reshape(a.shape[0], NX, NY, NCORE, part).transpose(0, 3, 2, 1, 4)
    return a.reshape(a.shape[0], -1)


def fetch(weight, held, sems):
    parts = sems.shape[0]
    block = held.shape[0] // parts
    cuts = [slice(i * block, (i + 1) * block) for i in range(parts)]
    copies = [
        pltpu.make_async_copy(weight.at[cut], held.at[cut], sems.at[i])
        for i, cut in enumerate(cuts)
    ]
    for copy in copies:
        copy.start()
    return cuts, copies


def sent_kernel(act_other, grads, grads_other, weight, up, send, held, ready, sems, out_sems):
    cuts, copies = fetch(weight, held, sems)
    half, width = held.shape
    items = grads.shape[0] // 2
    both = jnp.concatenate([grads[...], grads_other[...]], axis=0)
    for cut, copy in zip(cuts, copies):
        copy.wait()
        back = dot(both, held[cut], 1, 1)
        row, column = divmod(cut.start, half // 2)
        row, to = row * items, slice(column, column + cut.stop - cut.start)
        up[row : row + items, to] = back[:items] + back[items : 2 * items]
        to = slice(width + to.start, width + to.stop)
        ready[row : row + items, to] = back[2 * items : 3 * items] + back[3 * items :]
    parts = out_sems.shape[0] - 1
    ends = [i * width // parts for i in range(parts + 1)] + [send.shape[1]]
    outs = [
        pltpu.make_async_copy(ready.at[:, lo:hi], send.at[:, lo:hi], out_sems.at[i])
        for i, (lo, hi) in enumerate(zip(ends[:-1], ends[1:]))
    ]
    outs[-1].start()
    for i in range(parts):
        at = slice(ends[i], ends[i + 1])
        ready[:, at] = dot(act_other[...], held[:, at])
        outs[i].start()
    for out in outs:
        out.wait()


def kept_kernel(act, weight, keep, held, sems):
    cuts, copies = fetch(weight, held, sems)
    total = None
    for cut, copy in zip(cuts, copies):
        copy.wait()
        part = dot(act[:, cut], held[cut])
        total = part if total is None else total + part
    keep[...] = total


def last_kernel(core, keep, sums, got, hidden, item_emb, item_gain, user_gain, values, item_grad, up):
    width = values.shape[1]
    items = hidden.shape[0]
    block = sums.shape[1]
    part = width // (NX * NY * NCORE)
    tile = part * NX
    values[...] = (keep[...] + got[:, :width]).astype(jnp.bfloat16)
    for side, ref, skip in ((core[0], sums, 0), (1 - core[0], got, width)):
        for piece in range(2):
            at = pl.multiple_of((2 * side + piece) * block, block)
            up[:, pl.ds(at, block)] = ref[piece * items : (piece + 1) * items, skip:]
    x = item_emb[...].astype(jnp.float32)
    scale = lax.rsqrt(jnp.mean(x * x, axis=1, keepdims=True) + eps)
    emb_grad = norm_back(x, user_gain[...], scale, up[...])
    hid = hidden[...].astype(jnp.float32)
    scale = lax.rsqrt(jnp.mean(hid * hid, axis=1, keepdims=True) + eps)
    up[...] = norm_back(hid, item_gain[...], scale, emb_grad)
    group = lax.broadcasted_iota(jnp.int32, (items, tile), 1) // part
    for out in range(width // tile):
        at_x, y = out // (NY // 2), 2 * (out % (NY // 2))
        total = None
        for to, (side, at_y) in enumerate(((0, y), (1, y), (0, y + 1), (1, y + 1))):
            piece = up[:, (side * NY + at_y) * tile : (side * NY + at_y + 1) * tile]
            piece = pltpu.roll(piece, (to - at_x) % NX * part, 1)
            total = piece if total is None else jnp.where(group == to, piece, total)
        item_grad[:, out * tile : (out + 1) * tile] = total


def local(item_hidden, item_gain, history, owner_map, user_gain, value_weight, value_grad):
    groups = lax.axis_size("dp")
    item_rows, width = item_hidden.shape
    hist_rows = history.shape[0]
    half = width // 2
    core = lax.axis_index("core")
    f32, bf16 = jnp.float32, jnp.bfloat16

    seed = lax.all_gather(value_weight, "x", axis=0, tiled=True)
    history, seed = lax.optimization_barrier((history, seed))
    weight = lax.all_gather(seed, "y", axis=0, tiled=True)

    pool = owner_map.shape[1]
    stored = locate(owner_map, history)
    pick = stored[:, None] == lax.broadcasted_iota(jnp.int32, (hist_rows, pool), 1)
    wanted = jnp.any(pick, axis=0).reshape(groups, item_rows)
    slot = jnp.cumsum(wanted.astype(jnp.int32), axis=1) - 1
    slot_pos = jnp.sum(jnp.where(pick, slot.reshape(1, pool), 0), axis=1)
    buffer_row = stored // item_rows * CAP + slot_pos
    one_hot = (
        buffer_row[:, None] == lax.broadcasted_iota(jnp.int32, (hist_rows, groups * CAP), 1)
    ).astype(bf16)
    grad_sums = dot(one_hot, value_grad, 0, 0).astype(bf16).reshape(groups, CAP, width)
    slot_ids = lax.broadcasted_iota(jnp.int32, (groups, CAP, item_rows), 1)
    asked = (wanted[:, None, :] & (slot[:, None, :] == slot_ids)).astype(bf16)
    asked = jnp.pad(asked, ((0, 0), (0, 0), (0, -item_rows % 128)))
    sent = jnp.concatenate([grad_sums, asked], axis=2)
    arrived = lax.all_to_all(sent, "dp", split_axis=0, concat_axis=0, tiled=True)
    arrived = arrived.reshape(groups * CAP, -1)
    select = arrived[:, width : width + item_rows]

    hidden = split(item_hidden)
    item_gain, user_gain = split(item_gain.reshape(1, width)), split(user_gain.reshape(1, width))
    item_emb, _ = norm_rows(hidden.astype(f32), item_gain)
    item_emb = item_emb.astype(bf16)
    outgoing = dot(select, item_emb).astype(bf16).reshape(groups, CAP, width)
    incoming = lax.all_to_all(outgoing, "dp", split_axis=0, concat_axis=0, tiled=True)

    swap = [(0, 1), (1, 0)]
    total = dot(select, arrived[:, :width], 0, 0)
    high = lax.reduce_precision(total, 8, 7)
    grads = jnp.concatenate([high, total - high], axis=0).astype(bf16)
    grads_other = lax.ppermute(grads, "core", swap)
    normed, _ = norm_rows(incoming.reshape(groups * CAP, width).astype(f32), user_gain)
    normed = dot(one_hot, normed.astype(bf16)).astype(bf16)
    low, high = normed[:, :half], normed[:, half:]
    act = jnp.where(core == 0, low, high)
    act_other = lax.ppermute(jnp.where(core == 0, high, low), "core", swap)

    vmem = pl.BlockSpec(memory_space=pltpu.VMEM)
    hbm = pl.BlockSpec(memory_space=pltpu.HBM)
    extra = half * item_rows // hist_rows
    held = [pltpu.VMEM((half, width), bf16)]
    flops = 2 * hist_rows * half * width
    sums, send = pl.pallas_call(
        sent_kernel,
        out_shape=[
            jax.ShapeDtypeStruct((hist_rows, extra), f32),
            jax.ShapeDtypeStruct((hist_rows, width + extra), f32),
        ],
        in_specs=[vmem] * 3 + [hbm],
        out_specs=[vmem, hbm],
        scratch_shapes=held
        + [
            pltpu.VMEM((hist_rows, width + extra), f32),
            pltpu.SemaphoreType.DMA((2,)),
            pltpu.SemaphoreType.DMA((5,)),
        ],
        cost_estimate=pl.CostEstimate(flops=3 * flops, bytes_accessed=6 << 20, transcendentals=0),
        compiler_params=pltpu.CompilerParams(vmem_limit_bytes=52 << 20),
    )(act_other, grads, grads_other, weight)
    got = lax.ppermute(send, "core", swap)
    (keep,) = pl.pallas_call(
        kept_kernel,
        out_shape=[jax.ShapeDtypeStruct((hist_rows, width), f32)],
        in_specs=[vmem, hbm],
        out_specs=[vmem],
        scratch_shapes=held + [pltpu.SemaphoreType.DMA((4,))],
        cost_estimate=pl.CostEstimate(flops=flops, bytes_accessed=5 << 20, transcendentals=0),
        compiler_params=pltpu.CompilerParams(vmem_limit_bytes=52 << 20),
    )(act, weight)
    values, item_grad = pl.pallas_call(
        last_kernel,
        out_shape=[
            jax.ShapeDtypeStruct((hist_rows, width), bf16),
            jax.ShapeDtypeStruct((item_rows, width), f32),
        ],
        in_specs=[pl.BlockSpec(memory_space=pltpu.SMEM)] + [vmem] * 7,
        out_specs=[vmem] * 2,
        scratch_shapes=[pltpu.VMEM((item_rows, width), f32)],
        compiler_params=pltpu.CompilerParams(vmem_limit_bytes=12 << 20),
    )(core.reshape(1).astype(jnp.int32), keep, sums, got, hidden, item_emb, item_gain, user_gain)
    return (values, item_grad)


def solution(mesh):
    groups = mesh.shape["dp"]
    mesh = Mesh(mesh.devices.reshape(groups, NX, NY, NCORE), ("dp",) + ROW)
    everywhere = ("dp",) + ROW
    in_specs = (
        P(everywhere, None),
        P(),
        P(everywhere),
        P(ROW, None),
        P(),
        P(ROW, None),
        P(everywhere, None),
    )
    out_specs = (P(everywhere, None), P(everywhere, None))
    return jax.shard_map(local, mesh=mesh, in_specs=in_specs, out_specs=out_specs, check_vma=False)
```

```python
import jax
import jax.numpy as jnp
from jax import lax
from jax.experimental import pallas as pl
from jax.experimental.pallas import tpu as pltpu
from jax.sharding import Mesh, PartitionSpec as P

CAP = 8
NX, NY, NCORE = 4, 8, 2
ROW = ("x", "y", "core")


eps = 1e-06


def norm_rows(values, gain):
    scale = lax.rsqrt(jnp.mean(values * values, axis=1, keepdims=True) + eps)
    return (values * scale * gain, scale)


def norm_back(values, gain, scale, upstream):
    unit = values * scale
    scaled = upstream * gain
    return scale * (scaled - unit * jnp.mean(scaled * unit, axis=1, keepdims=True))


def locate(owner_row, items):
    matches = items[:, None] == lax.broadcasted_iota(
        jnp.int32, (items.shape[0], owner_row.shape[1]), 1
    )
    return jnp.sum(jnp.where(matches, owner_row, 0), axis=1)


def dot(a, b, da=1, db=0):
    return lax.dot_general(a, b, (((da,), (db,)), ((), ())), preferred_element_type=jnp.float32)


def split(a):
    part = a.shape[1] // (NX * NY * NCORE)
    a = a.reshape(a.shape[0], NX, NY, NCORE, part).transpose(0, 3, 2, 1, 4)
    return a.reshape(a.shape[0], -1)


def fetch(weight, held, sems):
    parts = sems.shape[0]
    block = held.shape[0] // parts
    cuts = [slice(i * block, (i + 1) * block) for i in range(parts)]
    copies = [
        pltpu.make_async_copy(weight.at[cut], held.at[cut], sems.at[i])
        for i, cut in enumerate(cuts)
    ]
    for copy in copies:
        copy.start()
    return cuts, copies


def sent_kernel(act_other, grads, grads_other, weight, up, send, held, ready, sems, out_sems):
    cuts, copies = fetch(weight, held, sems)
    half, width = held.shape
    items = grads.shape[0] // 2
    both = jnp.concatenate([grads[...], grads_other[...]], axis=0)
    for cut, copy in zip(cuts, copies):
        copy.wait()
        back = dot(both, held[cut], 1, 1)
        row, column = divmod(cut.start, half // 2)
        row, to = row * items, slice(column, column + cut.stop - cut.start)
        up[row : row + items, to] = back[:items] + back[items : 2 * items]
        to = slice(width + to.start, width + to.stop)
        ready[row : row + items, to] = back[2 * items : 3 * items] + back[3 * items :]
    parts = out_sems.shape[0] - 1
    ends = [i * width // parts for i in range(parts + 1)] + [send.shape[1]]
    outs = [
        pltpu.make_async_copy(ready.at[:, lo:hi], send.at[:, lo:hi], out_sems.at[i])
        for i, (lo, hi) in enumerate(zip(ends[:-1], ends[1:]))
    ]
    outs[-1].start()
    for i in range(parts):
        at = slice(ends[i], ends[i + 1])
        ready[:, at] = dot(act_other[...], held[:, at])
        outs[i].start()
    for out in outs:
        out.wait()


def kept_kernel(act, weight, keep, held, sems):
    cuts, copies = fetch(weight, held, sems)
    total = None
    for cut, copy in zip(cuts, copies):
        copy.wait()
        part = dot(act[:, cut], held[cut])
        total = part if total is None else total + part
    keep[...] = total


def last_kernel(
    core, keep, sums, got, hidden, item_emb, item_scale, scale, item_gain, user_gain,
    values, item_grad, ready, up, placed, sems,
):
    items, width = placed.shape
    block = sums.shape[1]
    part = width // (NX * NY * NCORE)
    tile = part * NX
    ready[...] = (keep[...] + got[:, :width]).astype(jnp.bfloat16)
    copies = [pltpu.make_async_copy(ready, values, sems.at[0])]
    copies[0].start()
    for side, ref, skip in ((core[0], sums, 0), (1 - core[0], got, width)):
        for piece in range(2):
            at = pl.multiple_of((2 * side + piece) * block, block)
            up[:, pl.ds(at, block)] = ref[piece * items : (piece + 1) * items, skip:]
    emb_grad = norm_back(item_emb[...].astype(jnp.float32), user_gain[...], scale[...], up[...])
    up[...] = norm_back(hidden[...].astype(jnp.float32), item_gain[...], item_scale[...], emb_grad)
    group = lax.broadcasted_iota(jnp.int32, (items, tile), 1) // part
    outs = width // tile
    for out in range(outs):
        at_x, y = out // (NY // 2), 2 * (out % (NY // 2))
        total = None
        for to, (side, at_y) in enumerate(((0, y), (1, y), (0, y + 1), (1, y + 1))):
            piece = up[:, (side * NY + at_y) * tile : (side * NY + at_y + 1) * tile]
            piece = pltpu.roll(piece, (to - at_x) % NX * part, 1)
            total = piece if total is None else jnp.where(group == to, piece, total)
        placed[:, out * tile : (out + 1) * tile] = total
        if out % (outs // 2) == outs // 2 - 1:
            half = slice(out // (outs // 2) * (width // 2), (out + 1) * tile)
            copies.append(
                pltpu.make_async_copy(
                    placed.at[:, half], item_grad.at[:, half], sems.at[len(copies)]
                )
            )
            copies[-1].start()
    for copy in copies:
        copy.wait()


def local(item_hidden, item_gain, history, owner_map, user_gain, value_weight, value_grad):
    groups = lax.axis_size("dp")
    item_rows, width = item_hidden.shape
    hist_rows = history.shape[0]
    half = width // 2
    core = lax.axis_index("core")
    f32, bf16 = jnp.float32, jnp.bfloat16

    seed = lax.all_gather(value_weight, "x", axis=0, tiled=True)
    history, seed = lax.optimization_barrier((history, seed))
    weight = lax.all_gather(seed, "y", axis=0, tiled=True)

    pool = owner_map.shape[1]
    stored = locate(owner_map, history)
    pick = stored[:, None] == lax.broadcasted_iota(jnp.int32, (hist_rows, pool), 1)
    wanted = jnp.any(pick, axis=0).reshape(groups, item_rows)
    slot = jnp.cumsum(wanted.astype(jnp.int32), axis=1) - 1
    slot_pos = jnp.sum(jnp.where(pick, slot.reshape(1, pool), 0), axis=1)
    buffer_row = stored // item_rows * CAP + slot_pos
    one_hot = (
        buffer_row[:, None] == lax.broadcasted_iota(jnp.int32, (hist_rows, groups * CAP), 1)
    ).astype(bf16)
    grad_sums = dot(one_hot, value_grad, 0, 0).astype(bf16).reshape(groups, CAP, width)
    slot_ids = lax.broadcasted_iota(jnp.int32, (groups, CAP, item_rows), 1)
    asked = (wanted[:, None, :] & (slot[:, None, :] == slot_ids)).astype(bf16)
    asked = jnp.pad(asked, ((0, 0), (0, 0), (0, -item_rows % 128)))
    sent = jnp.concatenate([grad_sums, asked], axis=2)
    arrived = lax.all_to_all(sent, "dp", split_axis=0, concat_axis=0, tiled=True)
    arrived = arrived.reshape(groups * CAP, -1)
    select = arrived[:, width : width + item_rows]

    hidden = split(item_hidden)
    item_gain, user_gain = split(item_gain.reshape(1, width)), split(user_gain.reshape(1, width))
    item_emb, item_scale = norm_rows(hidden.astype(f32), item_gain)
    item_emb = item_emb.astype(bf16)
    _, scale = norm_rows(item_emb.astype(f32), user_gain)
    outgoing = dot(select, item_emb).astype(bf16).reshape(groups, CAP, width)
    incoming = lax.all_to_all(outgoing, "dp", split_axis=0, concat_axis=0, tiled=True)

    swap = [(0, 1), (1, 0)]
    total = dot(select, arrived[:, :width], 0, 0)
    high = lax.reduce_precision(total, 8, 7)
    grads = jnp.concatenate([high, total - high], axis=0).astype(bf16)
    grads_other = lax.ppermute(grads, "core", swap)
    normed, _ = norm_rows(incoming.reshape(groups * CAP, width).astype(f32), user_gain)
    normed = dot(one_hot, normed.astype(bf16)).astype(bf16)
    low, high = normed[:, :half], normed[:, half:]
    act = jnp.where(core == 0, low, high)
    act_other = lax.ppermute(jnp.where(core == 0, high, low), "core", swap)

    vmem = pl.BlockSpec(memory_space=pltpu.VMEM)
    hbm = pl.BlockSpec(memory_space=pltpu.HBM)
    extra = half * item_rows // hist_rows
    held = [pltpu.VMEM((half, width), bf16)]
    flops = 2 * hist_rows * half * width
    sums, send = pl.pallas_call(
        sent_kernel,
        out_shape=[
            jax.ShapeDtypeStruct((hist_rows, extra), f32),
            jax.ShapeDtypeStruct((hist_rows, width + extra), f32),
        ],
        in_specs=[vmem] * 3 + [hbm],
        out_specs=[vmem, hbm],
        scratch_shapes=held
        + [
            pltpu.VMEM((hist_rows, width + extra), f32),
            pltpu.SemaphoreType.DMA((2,)),
            pltpu.SemaphoreType.DMA((5,)),
        ],
        cost_estimate=pl.CostEstimate(flops=3 * flops, bytes_accessed=6 << 20, transcendentals=0),
        compiler_params=pltpu.CompilerParams(vmem_limit_bytes=52 << 20),
    )(act_other, grads, grads_other, weight)
    got = lax.ppermute(send, "core", swap)
    (keep,) = pl.pallas_call(
        kept_kernel,
        out_shape=[jax.ShapeDtypeStruct((hist_rows, width), f32)],
        in_specs=[vmem, hbm],
        out_specs=[vmem],
        scratch_shapes=held + [pltpu.SemaphoreType.DMA((4,))],
        cost_estimate=pl.CostEstimate(flops=flops, bytes_accessed=5 << 20, transcendentals=0),
        compiler_params=pltpu.CompilerParams(vmem_limit_bytes=52 << 20),
    )(act, weight)
    values, item_grad = pl.pallas_call(
        last_kernel,
        out_shape=[
            jax.ShapeDtypeStruct((hist_rows, width), bf16),
            jax.ShapeDtypeStruct((item_rows, width), f32),
        ],
        in_specs=[pl.BlockSpec(memory_space=pltpu.SMEM)] + [vmem] * 9,
        out_specs=[hbm] * 2,
        scratch_shapes=[
            pltpu.VMEM((hist_rows, width), bf16),
            pltpu.VMEM((item_rows, width), f32),
            pltpu.VMEM((item_rows, width), f32),
            pltpu.SemaphoreType.DMA((3,)),
        ],
        compiler_params=pltpu.CompilerParams(vmem_limit_bytes=12 << 20),
    )(
        core.reshape(1).astype(jnp.int32), keep, sums, got, hidden, item_emb, item_scale, scale,
        item_gain, user_gain,
    )
    return (values, item_grad)


def solution(mesh):
    groups = mesh.shape["dp"]
    mesh = Mesh(mesh.devices.reshape(groups, NX, NY, NCORE), ("dp",) + ROW)
    everywhere = ("dp",) + ROW
    in_specs = (
        P(everywhere, None),
        P(),
        P(everywhere),
        P(ROW, None),
        P(),
        P(ROW, None),
        P(everywhere, None),
    )
    out_specs = (P(everywhere, None), P(everywhere, None))
    return jax.shard_map(local, mesh=mesh, in_specs=in_specs, out_specs=out_specs, check_vma=False)
```

```python
import jax
import jax.numpy as jnp
from jax import lax
from jax.experimental import pallas as pl
from jax.experimental.pallas import tpu as pltpu
from jax.sharding import Mesh, PartitionSpec as P

CAP = 8
NX, NY, NCORE = 4, 8, 2
ROW = ("x", "y", "core")


eps = 1e-06


def norm_rows(values, gain):
    scale = lax.rsqrt(jnp.mean(values * values, axis=1, keepdims=True) + eps)
    return (values * scale * gain, scale)


def norm_back(values, gain, scale, upstream):
    unit = values * scale
    scaled = upstream * gain
    return scale * (scaled - unit * jnp.mean(scaled * unit, axis=1, keepdims=True))


def locate(owner_row, items):
    matches = items[:, None] == lax.broadcasted_iota(
        jnp.int32, (items.shape[0], owner_row.shape[1]), 1
    )
    return jnp.sum(jnp.where(matches, owner_row, 0), axis=1)


def dot(a, b, da=1, db=0):
    return lax.dot_general(a, b, (((da,), (db,)), ((), ())), preferred_element_type=jnp.float32)


def split(a):
    part = a.shape[1] // (NX * NY * NCORE)
    a = a.reshape(a.shape[0], NX, NY, NCORE, part).transpose(0, 3, 2, 1, 4)
    return a.reshape(a.shape[0], -1)


def fetch(weight, held, sems):
    parts = sems.shape[0]
    block = held.shape[0] // parts
    cuts = [slice(i * block, (i + 1) * block) for i in range(parts)]
    copies = [
        pltpu.make_async_copy(weight.at[cut], held.at[cut], sems.at[i])
        for i, cut in enumerate(cuts)
    ]
    for copy in copies:
        copy.start()
    return cuts, copies


def sent_kernel(act_other, grads, grads_other, weight, up, send, held, ready, sems, out_sems):
    cuts, copies = fetch(weight, held, sems)
    half, width = held.shape
    items = grads.shape[0]
    both = jnp.concatenate([grads[...], grads_other[...]], axis=0)
    for cut, copy in zip(cuts, copies):
        copy.wait()
        back = dot(both, held[cut], 1, 1)
        row, column = divmod(cut.start, half // 2)
        row, to = row * items, slice(column, column + cut.stop - cut.start)
        up[row : row + items, to] = back[:items]
        to = slice(width + to.start, width + to.stop)
        ready[row : row + items, to] = back[items:]
    parts = out_sems.shape[0] - 1
    ends = [i * width // parts for i in range(parts + 1)] + [send.shape[1]]
    outs = [
        pltpu.make_async_copy(ready.at[:, lo:hi], send.at[:, lo:hi], out_sems.at[i])
        for i, (lo, hi) in enumerate(zip(ends[:-1], ends[1:]))
    ]
    outs[-1].start()
    for i in range(parts):
        at = slice(ends[i], ends[i + 1])
        ready[:, at] = dot(act_other[...], held[:, at])
        outs[i].start()
    for out in outs:
        out.wait()


def kept_kernel(act, weight, keep, held, sems):
    cuts, copies = fetch(weight, held, sems)
    total = None
    for cut, copy in zip(cuts, copies):
        copy.wait()
        part = dot(act[:, cut], held[cut])
        total = part if total is None else total + part
    keep[...] = total


def last_kernel(core, keep, sums, got, hidden, item_emb, item_gain, user_gain, values, item_grad, up):
    width = values.shape[1]
    items = hidden.shape[0]
    block = sums.shape[1]
    part = width // (NX * NY * NCORE)
    tile = part * NX
    values[...] = (keep[...] + got[:, :width]).astype(jnp.bfloat16)
    for side, ref, skip in ((core[0], sums, 0), (1 - core[0], got, width)):
        for piece in range(2):
            at = pl.multiple_of((2 * side + piece) * block, block)
            up[:, pl.ds(at, block)] = ref[piece * items : (piece + 1) * items, skip:]
    x = item_emb[...].astype(jnp.float32)
    scale = lax.rsqrt(jnp.mean(x * x, axis=1, keepdims=True) + eps)
    emb_grad = norm_back(x, user_gain[...], scale, up[...])
    hid = hidden[...].astype(jnp.float32)
    scale = lax.rsqrt(jnp.mean(hid * hid, axis=1, keepdims=True) + eps)
    up[...] = norm_back(hid, item_gain[...], scale, emb_grad)
    group = lax.broadcasted_iota(jnp.int32, (items, tile), 1) // part
    for out in range(width // tile):
        at_x, y = out // (NY // 2), 2 * (out % (NY // 2))
        total = None
        for to, (side, at_y) in enumerate(((0, y), (1, y), (0, y + 1), (1, y + 1))):
            piece = up[:, (side * NY + at_y) * tile : (side * NY + at_y + 1) * tile]
            piece = pltpu.roll(piece, (to - at_x) % NX * part, 1)
            total = piece if total is None else jnp.where(group == to, piece, total)
        item_grad[:, out * tile : (out + 1) * tile] = total


def local(item_hidden, item_gain, history, owner_map, user_gain, value_weight, value_grad):
    groups = lax.axis_size("dp")
    item_rows, width = item_hidden.shape
    hist_rows = history.shape[0]
    half = width // 2
    core = lax.axis_index("core")
    f32, bf16 = jnp.float32, jnp.bfloat16

    seed = lax.all_gather(value_weight, "x", axis=0, tiled=True)
    history, seed = lax.optimization_barrier((history, seed))
    weight = lax.all_gather(seed, "y", axis=0, tiled=True)

    pool = owner_map.shape[1]
    stored = locate(owner_map, history)
    pick = stored[:, None] == lax.broadcasted_iota(jnp.int32, (hist_rows, pool), 1)
    wanted = jnp.any(pick, axis=0).reshape(groups, item_rows)
    slot = jnp.cumsum(wanted.astype(jnp.int32), axis=1) - 1
    slot_pos = jnp.sum(jnp.where(pick, slot.reshape(1, pool), 0), axis=1)
    buffer_row = stored // item_rows * CAP + slot_pos
    one_hot = (
        buffer_row[:, None] == lax.broadcasted_iota(jnp.int32, (hist_rows, groups * CAP), 1)
    ).astype(bf16)
    grad_sums = dot(one_hot, value_grad, 0, 0).astype(bf16).reshape(groups, CAP, width)
    slot_ids = lax.broadcasted_iota(jnp.int32, (groups, CAP, item_rows), 1)
    asked = (wanted[:, None, :] & (slot[:, None, :] == slot_ids)).astype(bf16)
    asked = jnp.pad(asked, ((0, 0), (0, 0), (0, -item_rows % 128)))
    sent = jnp.concatenate([grad_sums, asked], axis=2)
    arrived = lax.all_to_all(sent, "dp", split_axis=0, concat_axis=0, tiled=True)
    arrived = arrived.reshape(groups * CAP, -1)
    select = arrived[:, width : width + item_rows]

    hidden = split(item_hidden)
    item_gain, user_gain = split(item_gain.reshape(1, width)), split(user_gain.reshape(1, width))
    item_emb, _ = norm_rows(hidden.astype(f32), item_gain)
    item_emb = item_emb.astype(bf16)
    outgoing = dot(select, item_emb).astype(bf16).reshape(groups, CAP, width)
    incoming = lax.all_to_all(outgoing, "dp", split_axis=0, concat_axis=0, tiled=True)

    swap = [(0, 1), (1, 0)]
    total = dot(select, arrived[:, :width], 0, 0)
    grads = total.astype(bf16)
    grads_other = lax.ppermute(grads, "core", swap)
    normed, _ = norm_rows(incoming.reshape(groups * CAP, width).astype(f32), user_gain)
    normed = dot(one_hot, normed.astype(bf16)).astype(bf16)
    low, high = normed[:, :half], normed[:, half:]
    act = jnp.where(core == 0, low, high)
    act_other = lax.ppermute(jnp.where(core == 0, high, low), "core", swap)

    vmem = pl.BlockSpec(memory_space=pltpu.VMEM)
    hbm = pl.BlockSpec(memory_space=pltpu.HBM)
    extra = half * item_rows // hist_rows
    held = [pltpu.VMEM((half, width), bf16)]
    flops = 2 * hist_rows * half * width
    sums, send = pl.pallas_call(
        sent_kernel,
        out_shape=[
            jax.ShapeDtypeStruct((hist_rows, extra), f32),
            jax.ShapeDtypeStruct((hist_rows, width + extra), f32),
        ],
        in_specs=[vmem] * 3 + [hbm],
        out_specs=[vmem, hbm],
        scratch_shapes=held
        + [
            pltpu.VMEM((hist_rows, width + extra), f32),
            pltpu.SemaphoreType.DMA((2,)),
            pltpu.SemaphoreType.DMA((5,)),
        ],
        cost_estimate=pl.CostEstimate(flops=3 * flops, bytes_accessed=6 << 20, transcendentals=0),
        compiler_params=pltpu.CompilerParams(vmem_limit_bytes=52 << 20),
    )(act_other, grads, grads_other, weight)
    got = lax.ppermute(send, "core", swap)
    (keep,) = pl.pallas_call(
        kept_kernel,
        out_shape=[jax.ShapeDtypeStruct((hist_rows, width), f32)],
        in_specs=[vmem, hbm],
        out_specs=[vmem],
        scratch_shapes=held + [pltpu.SemaphoreType.DMA((4,))],
        cost_estimate=pl.CostEstimate(flops=flops, bytes_accessed=5 << 20, transcendentals=0),
        compiler_params=pltpu.CompilerParams(vmem_limit_bytes=52 << 20),
    )(act, weight)
    values, item_grad = pl.pallas_call(
        last_kernel,
        out_shape=[
            jax.ShapeDtypeStruct((hist_rows, width), bf16),
            jax.ShapeDtypeStruct((item_rows, width), f32),
        ],
        in_specs=[pl.BlockSpec(memory_space=pltpu.SMEM)] + [vmem] * 7,
        out_specs=[vmem] * 2,
        scratch_shapes=[pltpu.VMEM((item_rows, width), f32)],
        compiler_params=pltpu.CompilerParams(vmem_limit_bytes=12 << 20),
    )(core.reshape(1).astype(jnp.int32), keep, sums, got, hidden, item_emb, item_gain, user_gain)
    return (values, item_grad)


def solution(mesh):
    groups = mesh.shape["dp"]
    mesh = Mesh(mesh.devices.reshape(groups, NX, NY, NCORE), ("dp",) + ROW)
    everywhere = ("dp",) + ROW
    in_specs = (
        P(everywhere, None),
        P(),
        P(everywhere),
        P(ROW, None),
        P(),
        P(ROW, None),
        P(everywhere, None),
    )
    out_specs = (P(everywhere, None), P(everywhere, None))
    return jax.shard_map(local, mesh=mesh, in_specs=in_specs, out_specs=out_specs, check_vma=False)
```
